32 devices in a mesh: img: 8 (over z, y), head: 4 (over x, core).
Axes of the slice: x: 2, y: 2, z: 4, core: 2. Of those that a mesh axis runs over, the one named last changes fastest.
Arguments:
- tokens: bfloat16 [192, 197, 768], P(('img', 'head')), may hold values from -6 to 6
- slot_ids: int32 [192, 160], P(('img', 'head')), may hold values from 0 to 196, as said below
- counts: int32 [192], P(('img', 'head')), may hold values from 39 to 157
- w_qkv: bfloat16 [768, 2304], P(None, 'head'), may hold values from -0.21875 to 0.21875
- w_out: bfloat16 [768, 768], P('head'), may hold values from -0.875 to 0.875
- w_up: bfloat16 [768, 3072], replicated, may hold values from -0.21875 to 0.21875
- w_down: bfloat16 [3072, 768], replicated, may hold values from -0.109375 to 0.109375
- gain_one: float32 [768], replicated, may hold values from 0.5 to 1.5
- bias_one: float32 [768], replicated, may hold values from -2 to 2
- gain_two: float32 [768], replicated, may hold values from 0.5 to 1.5
- bias_two: float32 [768], replicated, may hold values from -2 to 2
- w_router: float32 [768], replicated, may hold values from -0.21875 to 0.21875
- cotangent: bfloat16 [192, 197, 768], P(('img', 'head')), may hold values from -6 to 6
Outputs:
- result: bfloat16 [192, 197, 768], P(('img', 'head'))
- grad_tokens: float32 [192, 197, 768], P(('img', 'head'))
- grad_qkv: float32 [768, 2304], P(None, 'head')
- grad_out: float32 [768, 768], P('head')
- grad_up: float32 [768, 3072], P(None, 'head')
- grad_down: float32 [3072, 768], P('head')
- grad_gain_one: float32 [768], P('head')
- grad_bias_one: float32 [768], P('head')
- grad_gain_two: float32 [768], P('head')
- grad_bias_two: float32 [768], P('head')
- grad_router: float32 [768], P('head')
The draws below stay inside these ranges and needn't reach their ends.
Inputs may be any that keep to these rules, and one draw needn't show every extreme that they name: `slot_ids`: within each image the 160 slots hold distinct token numbers; the first counts of them are the routed tokens.
All inputs are finite; a program needn't handle non-finite values.
Results may differ from the reference program's by a relative error of at most 0.012.
The reference program's roundings to bfloat16 on the way count: a program that leaves them out, or rounds other values in their place, can miss the bound.
Values may be sent and summed in bfloat16 or wider, within the bound.
A program may use at most 256 MiB of HBM per device.

```python
import jax
import jax.numpy as jnp
from jax import lax

D = 768
HEADS = 12
HEAD_DIM = 64
FF = 3072
SEQ = 197
CAP = 160
IMAGES = 192
LOSEL = 39
MAXSEL = 157


def draw_slot_ids(key, part):
    key = jax.random.fold_in(key, 11)
    image_keys = jax.random.split(key, IMAGES)
    orders = jax.vmap(lambda image_key: jax.random.permutation(image_key, SEQ))(image_keys)
    return orders[:, :CAP].astype(jnp.int32)


def draw_counts(key, part):
    key = jax.random.fold_in(key, 23)
    first_key, second_key = jax.random.split(key)
    chosen = jax.random.randint(first_key, (IMAGES,), LOSEL, MAXSEL + 1)
    placing = jax.random.permutation(second_key, IMAGES)
    chosen = chosen.at[placing[0]].set(MAXSEL).at[placing[1]].set(LOSEL)
    return chosen.astype(jnp.int32)


def levels(rng, extent, shards, smallest, top_value):
    level = 1.0
    for position, blocks in shards:
        draws = jax.random.uniform(jax.random.fold_in(jax.random.fold_in(rng, 6), position), (blocks,), jnp.float32, smallest / len(shards), top_value / len(shards))
        level = level * jnp.repeat(jnp.exp(draws), extent[position] // blocks).reshape((-1,) + (1,) * (len(extent) - 1 - position))
    return level


def noise(key, dims, spread, most, shards=(), kind=jnp.bfloat16):
    factor_of = levels(key, dims, shards, -0.22, 0.18) if shards else 1.0
    values = jax.random.normal(key, dims, jnp.float32) * spread * factor_of
    return jnp.minimum(jnp.maximum(values, -most), most).astype(kind)


def setup_inputs(seed: int = 0) -> dict:
    streams_of = jax.random.split(jax.random.key(seed), 14)
    tokens = noise(streams_of[0], (IMAGES, SEQ, D), 1.0, 6.0, ((0, 32),))
    slot_ids = draw_slot_ids(jax.random.fold_in(streams_of[13], 71), 0)
    counts = draw_counts(jax.random.fold_in(streams_of[13], 71), 0)
    w_qkv = noise(streams_of[3], (D, 3 * D), D ** -0.5, 0.21875, ((1, 4),))
    w_out = noise(streams_of[4], (D, D), (D // 16) ** -0.5, 0.875, ((0, 4),))
    w_up = noise(streams_of[5], (D, FF), D ** -0.5, 0.21875)
    w_down = noise(streams_of[6], (FF, D), FF ** -0.5, 0.109375)
    gain_one = jnp.clip(1.0 + 0.1 * jax.random.normal(streams_of[7], (D,), jnp.float32), 0.5, 1.5)
    bias_one = noise(streams_of[8], (D,), 0.3, 2.0, (), jnp.float32)
    gain_two = jnp.clip(1.0 + 0.1 * jax.random.normal(streams_of[9], (D,), jnp.float32), 0.5, 1.5)
    bias_two = noise(streams_of[10], (D,), 0.3, 2.0, (), jnp.float32)
    w_router = noise(streams_of[11], (D,), D ** -0.5, 0.21875, (), jnp.float32)
    cotangent = noise(streams_of[12], (IMAGES, SEQ, D), 1.0, 6.0, ((0, 32),))
    return dict(tokens=tokens, slot_ids=slot_ids, counts=counts, w_qkv=w_qkv, w_out=w_out, w_up=w_up, w_down=w_down, gain_one=gain_one, bias_one=bias_one, gain_two=gain_two, bias_two=bias_two, w_router=w_router, cotangent=cotangent)


@jax.custom_vjp
def low(v):
    return lax.optimization_barrier(v.astype(jnp.bfloat16)).astype(jnp.float32)

@jax.custom_vjp
def low_back(v):
    return v

def low_keep(v):
    return (low(v), None)

def low_pass(kept, grad):
    return (grad,)

def back_keep(v):
    return (v, None)

def back_low(kept, grad):
    return (low(grad),)
low.defvjp(low_keep, low_pass)
low_back.defvjp(back_keep, back_low)

def layer_norm(values, norm_gain, norm_bias):
    average = lax.optimization_barrier(jnp.mean(values, axis=-1, keepdims=True))
    centred = values - average
    variance = lax.optimization_barrier(jnp.mean(centred * centred, axis=-1, keepdims=True))
    return centred * lax.rsqrt(variance + 1e-06) * norm_gain + norm_bias

def gelu_exact(values):
    return jax.nn.gelu(values, approximate=False)

def select_rows(matrix, indices):
    return jax.vmap(lambda image_rows, positions: image_rows[positions])(matrix, indices)

def add_rows(matrix, indices, additions):
    return jax.vmap(lambda image_rows, positions, addend: image_rows.at[positions].add(addend))(matrix, indices, additions)

def forward(tokens, slot_ids, counts, w_qkv, w_out, w_up, w_down, gain_one, bias_one, gain_two, bias_two, w_router):
    precise = lax.Precision.HIGHEST
    images = tokens.shape[0]
    picked = select_rows(tokens, slot_ids)
    key_valid = jnp.arange(CAP)[None, :] < counts[:, None]
    slot_mask = key_valid.astype(jnp.float32)
    normed_one = low(layer_norm(picked, gain_one, bias_one))
    projected = low(low_back(jnp.einsum('icd,de->ice', normed_one, w_qkv, precision=precise)))
    projected = projected.reshape(images, CAP, HEADS, 3, HEAD_DIM)
    query_rows = projected[:, :, :, 0]
    key_rows = projected[:, :, :, 1]
    value_rows = projected[:, :, :, 2]
    scores = low_back(jnp.einsum('gqhe,gkhe->ghqk', query_rows, key_rows, precision=precise) * HEAD_DIM ** (-0.5))
    scores = jnp.where(key_valid[:, None, None, :], scores, -1e+30)
    probabilities = low(jax.nn.softmax(scores, axis=-1))
    mixed_heads = low(low_back(jnp.einsum('ghqk,gkhe->gqhe', probabilities, value_rows, precision=precise)))
    mixed_heads = mixed_heads.reshape(images, CAP, D)
    attn_out = low_back(jnp.einsum('ice,ed->icd', mixed_heads, w_out, precision=precise))
    hidden_in = picked + attn_out
    normed_two = low(layer_norm(hidden_in, gain_two, bias_two))
    pre_act = low_back(jnp.einsum('icd,df->icf', normed_two, w_up, precision=precise))
    activated = low(gelu_exact(pre_act))
    mlp_out = low_back(jnp.einsum('icf,fd->icd', activated, w_down, precision=precise))
    gate_value = jax.nn.sigmoid(lax.optimization_barrier(jnp.sum(picked * w_router, axis=-1)))
    weight_row = gate_value * slot_mask
    return add_rows(tokens, slot_ids, weight_row[..., None] * (attn_out + mlp_out))

def reference(tokens, slot_ids, counts, w_qkv, w_out, w_up, w_down, gain_one, bias_one, gain_two, bias_two, w_router, cotangent):
    params = tuple((weight.astype(jnp.float32) for weight in (w_qkv, w_out, w_up, w_down, gain_one, bias_one, gain_two, bias_two, w_router)))
    group_size = 16
    blocks = IMAGES // group_size

    def split_up(array):
        return array.reshape((blocks, group_size) + array.shape[1:])

    def one_block(running, block_items):
        block_tokens, block_slots, block_counts, block_grad = block_items

        def block_forward(values, *weights):
            return forward(values, block_slots, block_counts, *weights)
        output, pullback = jax.vjp(block_forward, block_tokens.astype(jnp.float32), *params)
        gradients = pullback(block_grad.astype(jnp.float32))
        running = tuple((kept + addend for kept, addend in zip(running, gradients[1:])))
        return (running, (output.astype(jnp.bfloat16), gradients[0]))
    starting = tuple((jnp.zeros_like(weight) for weight in params))
    running, (outputs, grad_tokens) = lax.scan(one_block, starting, (split_up(tokens), split_up(slot_ids), split_up(counts), split_up(cotangent)))
    return (outputs.reshape(IMAGES, SEQ, D), grad_tokens.reshape(IMAGES, SEQ, D)) + running
```

```python
import jax
import jax.numpy as jnp
from jax import lax
from jax.sharding import PartitionSpec as P

HEAD_DIM = 64


def layer_norm(values, norm_gain, norm_bias):
    average = jnp.mean(values, axis=-1, keepdims=True)
    centred = values - average
    variance = jnp.mean(centred * centred, axis=-1, keepdims=True)
    return centred * lax.rsqrt(variance + 1e-06) * norm_gain + norm_bias


def gelu_exact(values):
    return jax.nn.gelu(values, approximate=False)


def slot_matrix(indices, length):
    return (indices[:, :, None] == jnp.arange(length)[None, None, :]).astype(jnp.bfloat16)


def select_rows(matrix, chosen):
    return jnp.einsum("gcs,gsd->gcd", chosen, matrix, preferred_element_type=jnp.float32)


def spread_rows(chosen, additions):
    upper = lax.reduce_precision(additions, 8, 7)
    lower = additions - upper
    parts = [part.astype(jnp.bfloat16) for part in (upper, lower)]
    spread = [
        jnp.einsum("gcs,gcd->gsd", chosen, part, preferred_element_type=jnp.float32) for part in parts
    ]
    return spread[0] + spread[1]


def masked_scores(query_rows, key_rows, key_valid):
    score_scale = query_rows.shape[-1] ** (-0.5)
    scores = (
        jnp.einsum("gqhe,gkhe->ghqk", query_rows, key_rows, preferred_element_type=jnp.float32)
        * score_scale
    )
    return jnp.where(key_valid[:, None, None, :], scores, -1e30)


def attend_forward(normed, key_valid, w_qkv):
    images, capacity, features = normed.shape
    projected = jnp.dot(
        normed.reshape(images * capacity, features), w_qkv, preferred_element_type=jnp.float32
    ).astype(jnp.bfloat16)
    projected = projected.reshape(images, capacity, -1, 3, HEAD_DIM)
    query_rows = projected[:, :, :, 0]
    key_rows = projected[:, :, :, 1]
    value_rows = projected[:, :, :, 2]
    scores = masked_scores(query_rows, key_rows, key_valid)
    highest = jnp.max(scores, axis=-1, keepdims=True)
    expo_terms = jnp.exp(scores - highest)
    totals = jnp.sum(expo_terms, axis=-1, keepdims=True)
    weights_b = (expo_terms / totals).astype(jnp.bfloat16)
    mixed_heads = jnp.einsum(
        "ghqk,gkhe->gqhe", weights_b, value_rows, preferred_element_type=jnp.float32
    ).astype(jnp.bfloat16)
    log_totals = highest + jnp.log(totals)
    return (
        mixed_heads.reshape(images * capacity, -1),
        (query_rows, key_rows, value_rows, log_totals),
    )


def attend_backward(normed, key_valid, kept_state, grad_mixed):
    query_rows, key_rows, value_rows, log_totals = kept_state
    images, capacity, head_count, head_size = query_rows.shape
    score_scale = head_size ** (-0.5)
    probs_full = jnp.exp(masked_scores(query_rows, key_rows, key_valid) - log_totals)
    grad_heads = grad_mixed.reshape(images, capacity, head_count, head_size)
    grad_value = jnp.einsum(
        "ghqk,gqhe->gkhe",
        probs_full.astype(jnp.bfloat16),
        grad_heads,
        preferred_element_type=jnp.float32,
    )
    grad_probs = jnp.einsum(
        "gqhe,gkhe->ghqk", grad_heads, value_rows, preferred_element_type=jnp.float32
    )
    grad_scores = probs_full * (
        grad_probs - jnp.sum(probs_full * grad_probs, axis=-1, keepdims=True)
    )
    grad_scores = grad_scores.astype(jnp.bfloat16)
    grad_query = (
        jnp.einsum("ghqk,gkhe->gqhe", grad_scores, key_rows, preferred_element_type=jnp.float32)
        * score_scale
    )
    grad_key = (
        jnp.einsum("ghqk,gqhe->gkhe", grad_scores, query_rows, preferred_element_type=jnp.float32)
        * score_scale
    )
    grad_proj = (
        jnp.stack([grad_query, grad_key, grad_value], axis=3)
        .astype(jnp.bfloat16)
        .reshape(images * capacity, -1)
    )
    grad_wqkv_t = jnp.einsum(
        "rc,rd->cd",
        grad_proj,
        normed.reshape(images * capacity, -1),
        preferred_element_type=jnp.float32,
    )
    return (grad_proj, grad_wqkv_t)


def shards(
    tokens,
    slot_ids,
    counts,
    w_qkv,
    w_out,
    w_up,
    w_down,
    gain_one,
    bias_one,
    gain_two,
    bias_two,
    w_router,
    cotangent,
):
    owned, length, features = tokens.shape
    capacity = slot_ids.shape[1]
    own_rows = owned * capacity
    chosen = slot_matrix(slot_ids, length)
    picked = select_rows(tokens, chosen)
    own_valid = jnp.arange(capacity)[None, :] < counts[:, None]
    slot_mask = own_valid.astype(jnp.float32)
    normed_f, norm_pull = jax.vjp(layer_norm, picked, gain_one, bias_one)
    normed_one = normed_f.astype(jnp.bfloat16)
    w_qkv = lax.all_gather(w_qkv, "head", axis=1, tiled=True)
    w_out = lax.all_gather(w_out, "head", axis=0, tiled=True)
    mixed_heads, kept_state = attend_forward(normed_one, own_valid, w_qkv)
    attn_out = jnp.dot(mixed_heads, w_out, preferred_element_type=jnp.float32).reshape(
        owned, capacity, features
    )
    hidden_in = picked + attn_out
    normed_two_f, norm_two_pull = jax.vjp(layer_norm, hidden_in, gain_two, bias_two)
    normed_two = normed_two_f.astype(jnp.bfloat16).reshape(own_rows, features)
    pre_act = jnp.dot(normed_two, w_up, preferred_element_type=jnp.float32)
    activated, act_pull = jax.vjp(gelu_exact, pre_act)
    activated_b = activated.astype(jnp.bfloat16)
    mlp_out = jnp.dot(activated_b, w_down, preferred_element_type=jnp.float32).reshape(
        owned, capacity, features
    )
    gate_value = jax.nn.sigmoid(jnp.sum(picked * w_router, axis=-1))
    weight_row = gate_value * slot_mask
    branch = attn_out + mlp_out
    result = (
        tokens.astype(jnp.float32) + spread_rows(chosen, weight_row[..., None] * branch)
    ).astype(jnp.bfloat16)
    grad_picked_out = select_rows(cotangent, chosen)
    grad_branch = weight_row[..., None] * grad_picked_out
    grad_gate = slot_mask * jnp.sum(grad_picked_out * branch, axis=-1)
    grad_logits = grad_gate * gate_value * (1.0 - gate_value)
    grad_router = jnp.einsum("ic,icd->d", grad_logits, picked)
    grad_mlp = grad_branch.astype(jnp.bfloat16).reshape(own_rows, features)
    grad_down = jnp.einsum("rf,rd->fd", activated_b, grad_mlp, preferred_element_type=jnp.float32)
    grad_act = jnp.einsum("rd,fd->rf", grad_mlp, w_down, preferred_element_type=jnp.float32)
    grad_pre = act_pull(grad_act)[0].astype(jnp.bfloat16)
    grad_up_t = jnp.einsum("rf,rd->fd", grad_pre, normed_two, preferred_element_type=jnp.float32)
    grad_normed_two = jnp.einsum(
        "rf,df->rd", grad_pre, w_up, preferred_element_type=jnp.float32
    ).reshape(owned, capacity, features)
    grad_hidden, grad_gain_two, grad_bias_two = norm_two_pull(grad_normed_two)
    grad_attn_b = (grad_branch + grad_hidden).astype(jnp.bfloat16).reshape(own_rows, features)
    group_grad = grad_attn_b
    grad_mixed = jnp.einsum(
        "rd,ed->re", group_grad, w_out, preferred_element_type=jnp.float32
    ).astype(jnp.bfloat16)
    grad_wout = jnp.einsum("re,rd->ed", mixed_heads, group_grad, preferred_element_type=jnp.float32)
    grad_proj, grad_wqkv_t = attend_backward(normed_one, own_valid, kept_state, grad_mixed)
    grad_normed = jnp.einsum(
        "rc,dc->rd", grad_proj, w_qkv, preferred_element_type=jnp.float32
    ).reshape(owned, capacity, features)
    grad_picked, grad_gain_one, grad_bias_one = norm_pull(grad_normed)
    grad_rows = grad_picked + grad_hidden + grad_logits[..., None] * w_router
    grad_tokens = cotangent.astype(jnp.float32) + spread_rows(chosen, grad_rows)
    parts = lax.axis_size("head")
    me = lax.axis_index("head")

    def reduced(matrix):
        shard = lax.psum_scatter(
            matrix.astype(jnp.bfloat16), "head", scatter_dimension=0, tiled=True
        )
        piece = lax.psum_scatter(shard, "img", scatter_dimension=0, tiled=True)
        return lax.all_gather(piece, "img", axis=0, tiled=True).astype(jnp.float32)

    vectors = lax.psum(
        jnp.stack([grad_gain_one, grad_bias_one, grad_gain_two, grad_bias_two, grad_router]),
        ("img", "head"),
    )
    vectors = lax.dynamic_slice_in_dim(
        vectors, me * (features // parts), features // parts, axis=1
    )
    return (
        result,
        grad_tokens,
        reduced(grad_wqkv_t).T,
        reduced(grad_wout),
        reduced(grad_up_t).T,
        reduced(grad_down),
        vectors[0],
        vectors[1],
        vectors[2],
        vectors[3],
        vectors[4],
    )


def solution(mesh):
    return jax.shard_map(
        shards,
        mesh=mesh,
        in_specs=(
            P(("img", "head"), None, None),
            P(("img", "head"), None),
            P(("img", "head")),
            P(None, "head"),
            P("head", None),
            P(),
            P(),
            P(),
            P(),
            P(),
            P(),
            P(),
            P(("img", "head"), None, None),
        ),
        out_specs=(
            P(("img", "head"), None, None),
            P(("img", "head"), None, None),
            P(None, "head"),
            P("head", None),
            P(None, "head"),
            P("head", None),
            P("head"),
            P("head"),
            P("head"),
            P("head"),
            P("head"),
        ),
        check_vma=False,
    )
```

```python
import functools

import jax
import jax.numpy as jnp
from jax import lax
from jax.experimental import pallas as pl
from jax.experimental.pallas import tpu as pltpu
from jax.sharding import PartitionSpec as P

HEAD_DIM = 64
EPS = 1e-06
BF = jnp.bfloat16
F32 = jnp.float32


def nn(a, b):
    return lax.dot_general(a, b, (((1,), (0,)), ((), ())), preferred_element_type=F32)


def nt(a, b):
    return lax.dot_general(a, b, (((1,), (1,)), ((), ())), preferred_element_type=F32)


def tn(a, b):
    return lax.dot_general(a, b, (((0,), (0,)), ((), ())), preferred_element_type=F32)


def standardise(values):
    average = jnp.mean(values, axis=-1, keepdims=True)
    centred = values - average
    variance = jnp.mean(centred * centred, axis=-1, keepdims=True)
    scale = lax.rsqrt(variance + EPS)
    return centred * scale, scale


def norm_pull(grad, unit, scale, gain):
    inner = grad * gain
    first = jnp.mean(inner, axis=-1, keepdims=True)
    second = jnp.mean(inner * unit, axis=-1, keepdims=True)
    return scale * (inner - first - unit * second)


def split_low(values):
    upper = values.astype(BF)
    return upper, (values - upper.astype(F32)).astype(BF)


def slot_table(slots, length):
    capacity = slots.shape[1]
    return (lax.broadcasted_iota(jnp.int32, (length, capacity), 0) == slots).astype(BF)


def row_gate(picked, w_router, count):
    gate = jax.nn.sigmoid(jnp.sum(picked * w_router, axis=-1, keepdims=True))
    valid = (lax.broadcasted_iota(jnp.int32, gate.shape, 0) < count).astype(F32)
    return gate, valid


def lane_low(shape):
    return lax.broadcasted_iota(jnp.int32, shape, 1) < HEAD_DIM


def head_scores(key_tile, query_tile, low, count):
    scores = nt(key_tile, query_tile)
    seen = lax.broadcasted_iota(jnp.int32, scores.shape, 0) < count
    return jnp.where(seen, scores, -1e30)


def swap_halves(tile):
    return pltpu.roll(tile.astype(F32), HEAD_DIM, 1).astype(BF)


def pair_tiles(proj, rows, pair):
    base = pair * 6 * HEAD_DIM
    tiles = [proj[rows, base + 2 * HEAD_DIM * t : base + 2 * HEAD_DIM * (t + 1)] for t in range(3)]
    low = lane_low(tiles[0].shape)
    zero = jnp.zeros_like(tiles[0])
    swapped = [swap_halves(tile) for tile in tiles]
    scale = HEAD_DIM ** (-0.5)
    query_a = jnp.where(low, tiles[0], zero) * jnp.asarray(scale, BF)
    query_b = jnp.where(low, swapped[1], zero) * jnp.asarray(scale, BF)
    return tiles, swapped, low, zero, ((swapped[0], query_a), (tiles[2], query_b))


def copy_in(source, target, sem):
    copy = pltpu.make_async_copy(source, target, sem)
    copy.start()
    return copy


def fused_kernel(
    owned, length, capacity, parts,
    slots, counts, gain_one, bias_one, gain_two, bias_two, w_router,
    tokens, cotangent, w_all, w_up, w_down,
    result_o, grad_tokens_o, down_o, up_o, qkv_out_o, vec_o, saved_o,
    wu, wd, ra, rs, down, up, normed_two, grad_mlp, mixed, attn, wide, picked, picked_grad,
    totals, logits, tok, cot, res, gtok,
    sems, tok_sems, cot_sems, res_sems, gtok_sems,
):
    features, hidden = w_up.shape
    columns = w_all.shape[0] - features
    pairs = columns // (6 * HEAD_DIM)
    proj = ra.at[:, 0:columns]
    normed_one = ra.at[:, columns : columns + features]
    width = features // 3

    def rows_of(i):
        return pl.ds(pl.multiple_of(i * capacity, 16), capacity)

    load_w = copy_in(w_all, down, sems.at[0])
    load_up = copy_in(w_up, wu, sems.at[1])
    load_down = copy_in(w_down, wd, sems.at[2])

    def token_copy(i, slot):
        return pltpu.make_async_copy(tokens.at[i], tok.at[slot], tok_sems.at[slot])

    def cot_copy(i, slot):
        return pltpu.make_async_copy(cotangent.at[i], cot.at[slot], cot_sems.at[slot])

    token_copy(0, 0).start()
    cot_copy(0, 0).start()

    @pl.loop(0, owned)
    def _(i):
        slot = lax.rem(i, 2)

        @pl.when(i + 1 < owned)
        def _():
            token_copy(i + 1, 1 - slot).start()
            cot_copy(i + 1, 1 - slot).start()

        rows = rows_of(i)
        table = slot_table(slots[i], length)
        token_copy(i, slot).wait()
        rows_f = tn(table, tok[slot])
        picked[rows, :] = rows_f.astype(BF)
        unit, _ = standardise(rows_f)
        normed_one[rows, :] = (unit * gain_one[...] + bias_one[...]).astype(BF)
        gate, valid = row_gate(rows_f, w_router[...], counts[i])
        cot_copy(i, slot).wait()
        grads = tn(table, cot[slot])
        picked_grad[rows, :] = grads.astype(BF)
        grad_mlp[rows, :] = (gate * valid * grads).astype(BF)

    load_w.wait()
    for n in range(3):
        cols = slice(n * features, (n + 1) * features)
        proj[:, cols] = nt(normed_one[...], down[cols, :]).astype(BF)
    save = copy_in(ra, saved_o, sems.at[3])

    @pl.loop(0, owned)
    def _(i):
        rows = rows_of(i)
        for pair in range(pairs):
            tiles, swapped, low, zero, heads = pair_tiles(proj, rows, pair)
            outs = []
            for h, (key_tile, query_tile) in enumerate(heads):
                scores = head_scores(key_tile, query_tile, low, counts[i])
                highest = jnp.max(scores, axis=0, keepdims=True)
                terms = jnp.exp(scores - highest)
                total = jnp.sum(terms, axis=0, keepdims=True)
                probs = (terms * (1.0 / total)).astype(BF)
                totals[i, 2 * pair + h : 2 * pair + h + 1, :] = highest + jnp.log(total)
                outs.append(tn(probs, tiles[1 + h]))
            mixed[rows, 2 * HEAD_DIM * pair : 2 * HEAD_DIM * (pair + 1)] = jnp.where(
                low, outs[0], outs[1]
            ).astype(BF)

    for n in range(3):
        cols = slice(n * width, (n + 1) * width)
        attn[:, cols] = nn(mixed[...], down[columns : columns + features, cols])

    @pl.loop(0, owned)
    def _(i):
        rows = rows_of(i)
        unit, _ = standardise(picked[rows, :].astype(F32) + attn[rows, :])
        normed_two[rows, :] = (unit * gain_two[...] + bias_two[...]).astype(BF)

    save.wait()
    load_up.wait()
    step = hidden // 6

    @pl.loop(0, 6)
    def _(n):
        cols = pl.ds(pl.multiple_of(n * step, 128), step)
        pre = nn(normed_two[...], wu[:, cols])
        below = 0.5 + 0.5 * lax.erf(pre * (0.5**0.5))
        ra[:, cols] = (pre * below).astype(BF)
        rs[:, cols] = (below + pre * (jnp.exp(-0.5 * pre * pre) * 0.3989422804014327)).astype(BF)

    @pl.loop(0, 6)
    def _(n):
        cols = pl.ds(pl.multiple_of(n * step, 128), step)
        down[cols, :] = tn(ra[:, cols], grad_mlp[...]).astype(BF)

    put_down = copy_in(down, down_o, sems.at[4])
    load_down.wait()

    @pl.loop(0, 6)
    def _(n):
        cols = pl.ds(pl.multiple_of(n * step, 128), step)
        rs[:, cols] = (nt(grad_mlp[...], wd[cols, :]) * rs[:, cols].astype(F32)).astype(BF)

    @pl.loop(0, parts)
    def _(h):
        cols = pl.ds(pl.multiple_of(h * (hidden // parts), 128), hidden // parts)
        up[:, cols] = tn(normed_two[...], rs[:, cols]).astype(BF)

    put_up = copy_in(up, up_o, sems.at[5])

    for n in range(3):
        cols = slice(n * width, (n + 1) * width)
        wide[:, cols] = nn(ra[...], wd[:, cols]) + attn[:, cols]

    reload = copy_in(saved_o, ra, sems.at[3])
    vec_o[...] = jnp.zeros_like(vec_o)

    def result_copy(i, slot):
        return pltpu.make_async_copy(res.at[slot], result_o.at[i], res_sems.at[slot])

    def gtok_copy(i, slot):
        return pltpu.make_async_copy(gtok.at[slot], grad_tokens_o.at[i], gtok_sems.at[slot])

    token_copy(0, 0).start()

    @pl.loop(0, owned)
    def _(i):
        slot = lax.rem(i, 2)

        @pl.when(i + 1 < owned)
        def _():
            token_copy(i + 1, 1 - slot).start()

        rows = rows_of(i)
        rows_f = picked[rows, :].astype(F32)
        gate, valid = row_gate(rows_f, w_router[...], counts[i])
        branch = wide[rows, :]
        logit = valid * gate * (1.0 - gate) * jnp.sum(
            picked_grad[rows, :].astype(F32) * branch, axis=-1, keepdims=True
        )
        logits[rows, :] = jnp.broadcast_to(logit, (capacity, 128))
        vec_o[4:5, :] += jnp.sum(logit * rows_f, axis=0, keepdims=True)
        table = slot_table(slots[i], length)
        upper, lower = split_low(gate * valid * branch)
        token_copy(i, slot).wait()

        @pl.when(i >= 2)
        def _():
            result_copy(i - 2, slot).wait()

        res[slot] = (tok[slot].astype(F32) + (nn(table, upper) + nn(table, lower))).astype(BF)
        result_copy(i, slot).start()

    for n in range(3):
        cols = slice(n * width, (n + 1) * width)
        wide[:, cols] = nt(rs[...], wu[cols, :])

    blocks = [copy_in(w_all.at[columns : columns + features], rs.at[0:features, 0:features], sems.at[6])]
    for n in range(3):
        blocks.append(
            copy_in(
                w_all.at[n * features : (n + 1) * features],
                rs.at[0:features, (n + 1) * features : (n + 2) * features],
                sems.at[7 + n],
            )
        )

    @pl.loop(0, owned)
    def _(i):
        rows = rows_of(i)
        rows_f = picked[rows, :].astype(F32)
        unit, scale = standardise(rows_f + attn[rows, :])
        grad = wide[rows, :]
        vec_o[2:3, :] += jnp.sum(grad * unit, axis=0, keepdims=True)
        vec_o[3:4, :] += jnp.sum(grad, axis=0, keepdims=True)
        back = norm_pull(grad, unit, scale, gain_two[...])
        wide[rows, :] = back
        gate, valid = row_gate(rows_f, w_router[...], counts[i])
        grad_mlp[rows, :] = (gate * valid * picked_grad[rows, :].astype(F32) + back).astype(BF)

    wd[columns : columns + features, :] = tn(mixed[...], grad_mlp[...]).astype(BF)
    blocks[0].wait()
    normed_two[...] = nt(grad_mlp[...], rs[0:features, 0:features]).astype(BF)
    reload.wait()

    @pl.loop(0, owned)
    def _(i):
        rows = rows_of(i)
        for pair in range(pairs):
            tiles, swapped, low, zero, heads = pair_tiles(proj, rows, pair)
            lanes = slice(2 * HEAD_DIM * pair, 2 * HEAD_DIM * (pair + 1))
            grads = normed_two[rows, lanes]
            halves = (jnp.where(low, grads, zero), jnp.where(low, zero, grads))
            found = []
            for h, (key_tile, query_tile) in enumerate(heads):
                scores = head_scores(key_tile, query_tile, low, counts[i])
                probs = jnp.exp(scores - totals[i, 2 * pair + h : 2 * pair + h + 1, :])
                grad_probs = nt(tiles[1 + h], halves[h])
                shift = jnp.sum(probs * grad_probs, axis=0, keepdims=True)
                grad_scores = (probs * (grad_probs - shift)).astype(BF)
                grad_value = nn(probs.astype(BF), grads)
                scale = HEAD_DIM ** (-0.5)
                if h == 0:
                    grad_query = tn(grad_scores, swapped[0]) * scale
                    grad_key = nn(grad_scores, swapped[0]) * scale
                else:
                    grad_query = tn(grad_scores, swapped[2]) * scale
                    grad_key = nn(grad_scores, swapped[1]) * scale
                found.append((grad_query, grad_key, grad_value))
            (query_a, key_a, value_a), (query_b, key_b, value_b) = found
            base = pair * 6 * HEAD_DIM
            proj[rows, base : base + 128] = jnp.where(low, query_a, key_a).astype(BF)
            proj[rows, base + 128 : base + 256] = jnp.where(low, value_a, query_b).astype(BF)
            proj[rows, base + 256 : base + 384] = jnp.where(low, key_b, value_b).astype(BF)

    for n in range(3):
        cols = slice(n * features, (n + 1) * features)
        wd[cols, :] = tn(proj[:, cols], normed_one[...]).astype(BF)
    put_qkv = copy_in(wd, qkv_out_o, sems.at[6])

    for n in range(3):
        blocks[1 + n].wait()
    for n in range(3):
        cols = slice(n * width, (n + 1) * width)
        total = nn(proj[:, 0:features], rs[0:features, features + n * width : features + (n + 1) * width])
        for k in range(1, 3):
            base = (k + 1) * features + n * width
            total += nn(proj[:, k * features : (k + 1) * features], rs[0:features, base : base + width])
        attn[:, cols] = total

    cot_copy(0, 0).start()

    @pl.loop(0, owned)
    def _(i):
        slot = lax.rem(i, 2)

        @pl.when(i + 1 < owned)
        def _():
            cot_copy(i + 1, 1 - slot).start()

        rows = rows_of(i)
        rows_f = picked[rows, :].astype(F32)
        unit, scale = standardise(rows_f)
        grad = attn[rows, :]
        vec_o[0:1, :] += jnp.sum(grad * unit, axis=0, keepdims=True)
        vec_o[1:2, :] += jnp.sum(grad, axis=0, keepdims=True)
        back = norm_pull(grad, unit, scale, gain_one[...])
        total = back + wide[rows, :] + logits[rows, 0:1] * w_router[...]
        table = slot_table(slots[i], length)
        upper, lower = split_low(total)
        cot_copy(i, slot).wait()

        @pl.when(i >= 2)
        def _():
            gtok_copy(i - 2, slot).wait()

        gtok[slot] = cot[slot].astype(F32) + (nn(table, upper) + nn(table, lower))
        gtok_copy(i, slot).start()

    for i in range(max(owned - 2, 0), owned):
        result_copy(i, i % 2).wait()
        gtok_copy(i, i % 2).wait()
    put_down.wait()
    put_up.wait()
    put_qkv.wait()


def fused(
    parts, tokens, slot_ids, counts, w_all, w_up, w_down,
    gain_one, bias_one, gain_two, bias_two, w_router, cotangent,
):
    owned, length, features = tokens.shape
    capacity = slot_ids.shape[1]
    rows = owned * capacity
    hidden = w_up.shape[1]
    columns = w_all.shape[0] - features
    heads = columns // (3 * HEAD_DIM)
    slots = slot_ids.reshape(owned, 1, capacity)
    vectors = [v.reshape(1, features) for v in (gain_one, bias_one, gain_two, bias_two, w_router)]
    S = jax.ShapeDtypeStruct
    inside = pl.BlockSpec(memory_space=pltpu.VMEM)
    outside = pl.BlockSpec(memory_space=pltpu.HBM)
    scalars = pl.BlockSpec(memory_space=pltpu.SMEM)
    V = pltpu.VMEM
    return pl.pallas_call(
        functools.partial(fused_kernel, owned, length, capacity, parts),
        out_shape=[
            S((owned, length, features), BF), S((owned, length, features), F32),
            S((hidden, features), BF), S((features, hidden), BF), S((columns + features, features), BF),
            S((8, features), F32), S((rows, columns + features), BF),
        ],
        in_specs=[inside, scalars] + [inside] * 5 + [outside] * 5,
        out_specs=[outside] * 5 + [inside, outside],
        scratch_shapes=[
            V((features, hidden), BF), V((hidden, features), BF), V((rows, hidden), BF),
            V((rows, hidden), BF), V((hidden, features), BF), V((features, hidden), BF),
            V((rows, features), BF), V((rows, features), BF), V((rows, features), BF),
            V((rows, features), F32), V((rows, features), F32), V((rows, features), BF),
            V((rows, features), BF), V((owned, heads, capacity), F32), V((rows, 128), F32),
            V((2, length, features), BF), V((2, length, features), BF), V((2, length, features), BF),
            V((2, length, features), F32),
            pltpu.SemaphoreType.DMA((10,)), pltpu.SemaphoreType.DMA((2,)), pltpu.SemaphoreType.DMA((2,)),
            pltpu.SemaphoreType.DMA((2,)), pltpu.SemaphoreType.DMA((2,)),
        ],
        compiler_params=pltpu.CompilerParams(vmem_limit_bytes=62 << 20),
    )(slots, counts, *vectors, tokens, cotangent, w_all, w_up, w_down)


def shards(
    tokens,
    slot_ids,
    counts,
    w_qkv,
    w_out,
    w_up,
    w_down,
    gain_one,
    bias_one,
    gain_two,
    bias_two,
    w_router,
    cotangent,
):
    features = tokens.shape[2]
    parts = lax.axis_size("head")
    me = lax.axis_index("head")
    w_all = jnp.concatenate(
        [
            lax.all_gather(w_qkv.T, "head", axis=0, tiled=True),
            lax.all_gather(w_out, "head", axis=0, tiled=True),
        ]
    )
    result, grad_tokens, down, up, both, vectors, _ = fused(
        parts, tokens, slot_ids, counts, w_all, w_up, w_down,
        gain_one, bias_one, gain_two, bias_two, w_router, cotangent,
    )
    columns = w_all.shape[0] - features

    def reduced(matrix, axis=0):
        shard = lax.psum_scatter(matrix, "head", scatter_dimension=axis, tiled=True)
        piece = lax.psum_scatter(shard, "img", scatter_dimension=0, tiled=True)
        return lax.all_gather(piece, "img", axis=0, tiled=True).astype(F32)

    vectors = lax.psum(vectors, ("img", "head"))
    vectors = lax.dynamic_slice_in_dim(
        vectors, me * (features // parts), features // parts, axis=1
    )
    return (
        result,
        grad_tokens,
        reduced(both[:columns]).T,
        reduced(both[columns:]),
        reduced(up, 1),
        reduced(down),
        vectors[0],
        vectors[1],
        vectors[2],
        vectors[3],
        vectors[4],
    )


def solution(mesh):
    return jax.shard_map(
        shards,
        mesh=mesh,
        in_specs=(
            P(("img", "head"), None, None),
            P(("img", "head"), None),
            P(("img", "head")),
            P(None, "head"),
            P("head", None),
            P(),
            P(),
            P(),
            P(),
            P(),
            P(),
            P(),
            P(("img", "head"), None, None),
        ),
        out_specs=(
            P(("img", "head"), None, None),
            P(("img", "head"), None, None),
            P(None, "head"),
            P("head", None),
            P(None, "head"),
            P("head", None),
            P("head"),
            P("head"),
            P("head"),
            P("head"),
            P("head"),
        ),
        check_vma=False,
    )
```

```python
import functools

import jax
import jax.numpy as jnp
from jax import lax
from jax.experimental import pallas as pl
from jax.experimental.pallas import tpu as pltpu
from jax.sharding import PartitionSpec as P

HEAD_DIM = 64
EPS = 1e-06
BF = jnp.bfloat16
F32 = jnp.float32


def nn(a, b):
    return lax.dot_general(a, b, (((1,), (0,)), ((), ())), preferred_element_type=F32)


def nt(a, b):
    return lax.dot_general(a, b, (((1,), (1,)), ((), ())), preferred_element_type=F32)


def tn(a, b):
    return lax.dot_general(a, b, (((0,), (0,)), ((), ())), preferred_element_type=F32)


def standardise(values):
    average = jnp.mean(values, axis=-1, keepdims=True)
    centred = values - average
    variance = jnp.mean(centred * centred, axis=-1, keepdims=True)
    scale = lax.rsqrt(variance + EPS)
    return centred * scale, scale


def norm_pull(grad, unit, scale, gain):
    inner = grad * gain
    first = jnp.mean(inner, axis=-1, keepdims=True)
    second = jnp.mean(inner * unit, axis=-1, keepdims=True)
    return scale * (inner - first - unit * second)


def split_low(values):
    upper = values.astype(BF)
    return upper, (values - upper.astype(F32)).astype(BF)


def slot_table(slots, length):
    capacity = slots.shape[1]
    return (lax.broadcasted_iota(jnp.int32, (length, capacity), 0) == slots).astype(BF)


def row_gate(picked, w_router, count):
    gate = jax.nn.sigmoid(jnp.sum(picked * w_router, axis=-1, keepdims=True))
    valid = (lax.broadcasted_iota(jnp.int32, gate.shape, 0) < count).astype(F32)
    return gate, valid


def lane_low(shape):
    return lax.broadcasted_iota(jnp.int32, shape, 1) < HEAD_DIM


def head_scores(key_tile, query_tile, low, count):
    scores = nt(key_tile, query_tile)
    seen = lax.broadcasted_iota(jnp.int32, scores.shape, 0) < count
    return jnp.where(seen, scores, -1e30)


def swap_halves(tile):
    return pltpu.roll(tile.astype(F32), HEAD_DIM, 1).astype(BF)


def pair_lanes(pair, t):
    return pl.ds(pl.multiple_of((3 * pair + t) * 2 * HEAD_DIM, 128), 2 * HEAD_DIM)


def pair_tiles(proj, rows, pair):
    tiles = [proj[rows, pair_lanes(pair, t)] for t in range(3)]
    low = lane_low(tiles[0].shape)
    zero = jnp.zeros_like(tiles[0])
    swapped = [swap_halves(tile) for tile in tiles]
    scale = HEAD_DIM ** (-0.5)
    query_a = jnp.where(low, tiles[0], zero) * jnp.asarray(scale, BF)
    query_b = jnp.where(low, swapped[1], zero) * jnp.asarray(scale, BF)
    return tiles, swapped, low, zero, ((swapped[0], query_a), (tiles[2], query_b))

MESH_ID = pl.DeviceIdType.MESH
JOB_ROWS = 192
AG_ROWS = 96


def copy_in(source, target, sem):
    copy = pltpu.make_async_copy(source, target, sem)
    copy.start()
    return copy


def aligned(start, size, unit=16):
    return pl.ds(pl.multiple_of(start, unit), size)


class Place:
    def __init__(self, outer):
        self.head = lax.axis_index("head")
        self.img = lax.axis_index("img")
        self.outer = outer
        self.x, self.c = self.head // 2, self.head % 2
        self.z, self.y = self.img // 2, self.img % 2
        self.own = self.head
        self.across = 2 * (1 - self.x) + self.c
        self.core_at = (self.img, 2 * self.x + 1 - self.c)
        self.x_at = (self.img, self.across)
        self.y_at = (2 * self.z + 1 - self.y, self.head)
        self.z_at = []
        self.z_of = []
        for k in range(1, outer):
            other = lax.rem(self.z + k, outer)
            self.z_of.append(other)
            self.z_at.append((2 * other + self.y, self.head))


def send(source, target, sems, index, device):
    copy = pltpu.make_async_remote_copy(
        src_ref=source,
        dst_ref=target,
        send_sem=sems[0].at[index],
        recv_sem=sems[1].at[index],
        device_id=device,
        device_id_type=MESH_ID,
    )
    copy.start()
    return copy


class Gather:
    def __init__(self, place, whole, w_qkv_t, w_out, sems, local_sems):
        self.p, self.whole, self.sems = place, whole, sems
        self.w = (w_qkv_t, w_out)
        self.sizes = (w_qkv_t.shape[0], w_out.shape[0])
        self.columns = 4 * self.sizes[0]
        self.local_sems = local_sems
        self.sent = []
        self.split = (self.sizes[0] // 2) // AG_ROWS
        self.steps = self.split + 1

    def part(self, shard, kind, first=0, size=None):
        base = shard * self.sizes[kind] + (self.columns if kind else 0) + first
        return self.whole.at[aligned(base, size or self.sizes[kind])]

    def piece(self, shard, side, t):
        kind = 1 if t == self.split else 0
        first = side * AG_ROWS if kind else (self.split * side + t) * AG_ROWS
        return self.part(shard, kind, first, AG_ROWS)

    def source(self, side, t):
        kind = 1 if t == self.split else 0
        first = side * AG_ROWS if kind else (self.split * side + t) * AG_ROWS
        return self.w[kind].at[aligned(first, AG_ROWS)]

    def begin(self):
        p, n = self.p, self.steps
        self.local = [copy_in(self.w[k], self.part(p.own, k), self.local_sems.at[k]) for k in range(2)]
        self.core = [
            send(self.w[k], self.part(p.own, k), self.sems, k, p.core_at) for k in range(2)
        ]
        self.over_x = [
            send(self.source(p.y, t), self.piece(p.own, p.y, t), self.sems, 2 + t, p.x_at) for t in range(n)
        ]
        self.sent = self.core + self.over_x
        self.over_y = []
        self.passed = []

    def own_half(self):
        for copy in self.local:
            copy.wait()
        for copy in self.core:
            copy.wait_recv()

    def forward_x(self, t):
        p, n = self.p, self.steps
        self.over_x[t].wait_recv()
        block = self.piece(p.across, p.y, t)
        self.over_y.append(send(block, block, self.sems, 2 + n + t, p.y_at))
        self.passed.append(send(block, block, self.sems, 2 + 2 * n + t, p.core_at))

    def forward_y(self, t):
        p, n = self.p, self.steps
        self.over_y[t].wait_recv()
        block = self.piece(p.across, 1 - p.y, t)
        self.passed.append(send(block, block, self.sems, 2 + 3 * n + t, p.core_at))

    def other_half(self):
        for copy in self.passed:
            copy.wait_recv()

    def close(self):
        for copy in self.sent + self.over_y + self.passed:
            copy.wait_send()


class Reduce:
    def __init__(self, place, blocks, out, buffers, sems, local_sem):
        self.p, self.blocks, self.out = place, blocks, out
        self.from_core, self.from_x, self.from_y, self.from_z = buffers
        self.core_sems, self.x_sems, self.y_sems, self.z_sems, self.az_sems, self.ay_sems = sems
        self.local_sem = local_sem
        self.jobs = len(blocks)
        self.sent = []
        self.kept = []
        self.core, self.over_x, self.over_y = {}, {}, {}
        self.over_z, self.all_z, self.all_y = {}, {}, {}
        self.half = out.shape[1] // 2
        self.quarter = JOB_ROWS // place.outer
        self.mine = aligned(place.y * self.half, self.half, 128)
        self.theirs = aligned((1 - place.y) * self.half, self.half, 128)

    def ready(self, j):
        p = self.p
        shards = [(1 - p.x), p.x]
        self.core[j] = [
            send(
                self.blocks[j](2 * xx + 1 - p.c), self.from_core.at[j, xx],
                self.core_sems, (j, n), p.core_at,
            )
            for n, xx in enumerate(shards)
        ]
        self.sent += self.core[j]

    def to_x(self, j):
        p = self.p
        self.core[j][0].wait_recv()
        block = self.blocks[j](p.across)
        block[...] = (block[...].astype(F32) + self.from_core[j, 1 - p.x].astype(F32)).astype(BF)
        self.over_x[j] = send(block, self.from_x.at[j], self.x_sems, j, p.x_at)
        self.sent.append(self.over_x[j])

    def to_y(self, j):
        p = self.p
        self.core[j][1].wait_recv()
        self.over_x[j].wait_recv()
        block = self.blocks[j](p.own)
        block[...] = (
            block[...].astype(F32) + self.from_core[j, p.x].astype(F32) + self.from_x[j].astype(F32)
        ).astype(BF)
        self.over_y[j] = send(block.at[:, self.theirs], self.from_y.at[j], self.y_sems, j, p.y_at)
        self.sent.append(self.over_y[j])

    def to_z(self, j):
        p = self.p
        self.over_y[j].wait_recv()
        block = self.blocks[j](p.own).at[:, self.mine]
        block[...] = (block[...].astype(F32) + self.from_y[j].astype(F32)).astype(BF)
        self.over_z[j] = [
            send(
                block.at[aligned(self.quarter * p.z_of[k], self.quarter)], self.from_z.at[j, k],
                self.z_sems, (j, k), p.z_at[k],
            )
            for k in range(p.outer - 1)
        ]
        self.sent += self.over_z[j]

    def place_of(self, j, z, lanes):
        return self.out.at[aligned(j * JOB_ROWS + self.quarter * z, self.quarter), lanes]

    def spread(self, j):
        p = self.p
        for copy in self.over_z[j]:
            copy.wait_recv()
        piece = self.blocks[j](p.own).at[aligned(self.quarter * p.z, self.quarter), self.mine]
        total = piece[...].astype(F32)
        for k in range(p.outer - 1):
            total += self.from_z[j, k].astype(F32)
        piece[...] = total.astype(BF)
        target = self.place_of(j, p.z, self.mine)
        self.kept.append(copy_in(piece, target, self.local_sem.at[j]))
        self.all_z[j] = [
            send(piece, target, self.az_sems, (j, k), p.z_at[k]) for k in range(p.outer - 1)
        ]
        self.all_y[j] = [send(piece, target, self.ay_sems, (j, 0), p.y_at)]
        self.sent += self.all_z[j] + self.all_y[j]

    def across_y(self, j):
        p = self.p
        for k in range(p.outer - 1):
            self.all_z[j][k].wait_recv()
            z = lax.rem(p.z + p.outer - 1 - k, p.outer)
            block = self.place_of(j, z, self.mine)
            copy = send(block, block, self.ay_sems, (j, k + 1), p.y_at)
            self.all_y[j].append(copy)
            self.sent.append(copy)

    def finish(self, j):
        for copy in self.all_y[j]:
            copy.wait_recv()

    def tick(self, t):
        for lag, step in enumerate((self.to_y, self.to_z, self.spread, self.across_y, self.finish)):
            j = t - lag
            if lag == 0 and j + 1 < self.jobs and (j + 1) in self.core and (j + 1) not in self.over_x:
                self.to_x(j + 1)
            if 0 <= j < self.jobs:
                step(j)

    def close(self):
        for copy in self.sent:
            copy.wait_send()
        for copy in self.kept:
            copy.wait()


def sum_vectors(place, vec, inbox, sems, sent):
    p = place
    partners = [p.core_at, p.x_at, p.y_at]
    bit = 1
    while bit < p.outer:
        low = lax.rem(p.z // bit, 2)
        partners.append((2 * (p.z + bit - 2 * bit * low) + p.y, p.head))
        bit *= 2
    count = len(partners)
    copies = []

    def stage(n):
        if n:
            copies[n - 1].wait_recv()
            vec[n] = vec[n - 1] + inbox[n - 1]
        if n < count:
            copies.append(send(vec.at[n], inbox.at[n], sems, n, partners[n]))
            sent.append(copies[n])

    return [functools.partial(stage, n) for n in range(count + 1)]


def fused_kernel(owned, length, capacity, parts, outer, names, *refs):
    r = dict(zip(names, refs))
    remote = outer > 0
    slots, counts, vectors = r["slots"], r["counts"], r["vectors"]
    gain_one, bias_one, gain_two, bias_two, w_router = (vectors[n : n + 1, :] for n in range(5))
    tokens, cotangent = r["tokens"], r["cotangent"]
    wu, wd, ra, rs, down = r["wu"], r["wd"], r["ra"], r["rs"], r["down"]
    normed_two, grad_mlp, mixed, attn, wide = (
        r[k] for k in ("normed_two", "grad_mlp", "mixed", "attn", "wide")
    )
    picked, picked_grad, totals, logits = (r[k] for k in ("picked", "picked_grad", "totals", "logits"))
    tok, cot, res, gtok = (r[k] for k in ("tok", "cot", "res", "gtok"))
    sems, tok_sems, cot_sems, res_sems, gtok_sems = (
        r[k] for k in ("sems", "tok_sems", "cot_sems", "res_sems", "gtok_sems")
    )
    result_o, grad_tokens_o, saved_o, vec_o = (
        r[k] for k in ("result_o", "grad_tokens_o", "saved_o", "vec_o")
    )
    vec = r["vec"]
    features, hidden = wu.shape
    columns = wd.shape[0] - features
    pairs = columns // (6 * HEAD_DIM)
    proj = ra.at[:, 0:columns]
    normed_one = ra.at[:, columns : columns + features]
    width = features // 3
    part = hidden // parts

    def rows_of(i):
        return aligned(i * capacity, capacity)

    def slot_row(i):
        return slots[pl.ds(i, 1), :]

    def token_copy(i, slot):
        return pltpu.make_async_copy(tokens.at[i], tok.at[slot], tok_sems.at[slot])

    def cot_copy(i, slot):
        return pltpu.make_async_copy(cotangent.at[i], cot.at[slot], cot_sems.at[slot])

    def result_copy(i, slot):
        return pltpu.make_async_copy(res.at[slot], result_o.at[i], res_sems.at[slot])

    def gtok_copy(i, slot):
        return pltpu.make_async_copy(gtok.at[slot], grad_tokens_o.at[i], gtok_sems.at[slot])

    token_copy(0, 0).start()
    cot_copy(0, 0).start()
    reduce = None
    if remote:
        place = Place(outer)
        barrier = pltpu.get_barrier_semaphore()
        partners = [place.core_at, place.x_at, place.y_at, *place.z_at]
        for partner in partners:
            pl.semaphore_signal(barrier, inc=1, device_id=partner, device_id_type=MESH_ID)
        pl.semaphore_wait(barrier, len(partners))
        gather = Gather(
            place, down, r["w_qkv_t"], r["w_out"], (r["ag_send"], r["ag_recv"]), r["local_sems"]
        )
        gather.begin()
        w_all = r["w_saved_o"]
        half_order = (place.x, 1 - place.x)

        def rows_block(ref, base, step):
            return lambda s: ref.at[aligned(s * step + base, JOB_ROWS)]

        def lanes_block(ref, base):
            return lambda s: ref.at[base : base + JOB_ROWS, aligned(s * part, part, 128)]

        blocks = [rows_block(down, JOB_ROWS * k, part) for k in range(part // JOB_ROWS)]
        blocks += [lanes_block(wu, JOB_ROWS * k) for k in range(features // JOB_ROWS)]
        blocks += [rows_block(wd, columns, JOB_ROWS)]
        blocks += [rows_block(wd, JOB_ROWS * k, columns // parts) for k in range(columns // parts // JOB_ROWS)]
        reduce = Reduce(
            place, blocks, r["grads_o"], [r[k] for k in ("from_core", "from_x", "from_y", "from_z")],
            [(r[k + "_send"], r[k + "_recv"]) for k in ("core", "x", "y", "z", "az", "ay")],
            r["kept_sems"],
        )
        job_down, job_up = part // JOB_ROWS, features // JOB_ROWS
    else:
        w_all = r["w_all"]
        load_w = copy_in(w_all, down, sems.at[0])
        half_order = (0, 1)
    load_up = copy_in(r["w_up"], wu, sems.at[1])
    load_down = copy_in(r["w_down"], wd, sems.at[2])
    ticks = [0]

    def tick():
        if remote:
            reduce.tick(ticks[0])
            ticks[0] += 1

    @pl.loop(0, owned)
    def _(i):
        slot = lax.rem(i, 2)

        @pl.when(i + 1 < owned)
        def _():
            token_copy(i + 1, 1 - slot).start()
            cot_copy(i + 1, 1 - slot).start()

        rows = rows_of(i)
        table = slot_table(slot_row(i), length)
        token_copy(i, slot).wait()
        rows_f = tn(table, tok[slot])
        picked[rows, :] = rows_f.astype(BF)
        unit, _ = standardise(rows_f)
        normed_one[rows, :] = (unit * gain_one + bias_one).astype(BF)
        gate, valid = row_gate(rows_f, w_router, counts[i])
        cot_copy(i, slot).wait()
        grads = tn(table, cot[slot])
        picked_grad[rows, :] = grads.astype(BF)
        grad_mlp[rows, :] = (gate * valid * grads).astype(BF)

    def project(half):
        base = half * (columns // 2)
        cut = (columns // 4 + 127) // 128 * 128
        for first, size in ((0, cut), (cut, columns // 2 - cut)):
            start = pl.multiple_of(base + first, 128)
            proj[:, pl.ds(start, size)] = nt(normed_one[...], down[pl.ds(start, size), :]).astype(BF)

    def attend(half, first, last):
        @pl.loop(first, last)
        def _(i):
            rows = rows_of(i)
            for p in range(pairs // 2):
                pair = half * (pairs // 2) + p
                tiles, swapped, low, zero, heads = pair_tiles(proj, rows, pair)
                outs = []
                for h, (key_tile, query_tile) in enumerate(heads):
                    scores = head_scores(key_tile, query_tile, low, counts[i])
                    highest = jnp.max(scores, axis=0, keepdims=True)
                    terms = jnp.exp(scores - highest)
                    total = jnp.sum(terms, axis=0, keepdims=True)
                    probs = (terms * (1.0 / total)).astype(BF)
                    totals[i, pl.ds(2 * pair + h, 1), :] = highest + jnp.log(total)
                    outs.append(tn(probs, tiles[1 + h]))
                mixed[rows, aligned(2 * HEAD_DIM * pair, 2 * HEAD_DIM, 128)] = jnp.where(
                    low, outs[0], outs[1]
                ).astype(BF)

    if remote:
        gather.forward_x(0)
        gather.own_half()
        project(half_order[0])
        gather.forward_x(1)
        cuts = [0, owned // 3, (2 * owned) // 3, owned]
        attend(half_order[0], cuts[0], cuts[1])
        gather.forward_x(2)
        gather.forward_y(0)
        attend(half_order[0], cuts[1], cuts[2])
        gather.forward_x(3)
        gather.forward_y(1)
        attend(half_order[0], cuts[2], cuts[3])
        gather.forward_y(2)
        gather.forward_y(3)
        gather.other_half()
        keep_w = copy_in(down, w_all, sems.at[0])
        project(half_order[1])
        save = copy_in(ra, saved_o, sems.at[3])
        attend(half_order[1], 0, owned)
    else:
        load_w.wait()
        project(0)
        project(1)
        save = copy_in(ra, saved_o, sems.at[3])
        attend(0, 0, owned)
        attend(1, 0, owned)

    for n in range(3):
        cols = slice(n * width, (n + 1) * width)
        attn[:, cols] = nn(mixed[...], down[columns : columns + features, cols])

    @pl.loop(0, owned)
    def _(i):
        rows = rows_of(i)
        unit, _ = standardise(picked[rows, :].astype(F32) + attn[rows, :])
        normed_two[rows, :] = (unit * gain_two + bias_two).astype(BF)

    save.wait()
    load_up.wait()
    step = hidden // 6

    @pl.loop(0, 6)
    def _(n):
        cols = aligned(n * step, step, 128)
        pre = nn(normed_two[...], wu[:, cols])
        below = 0.5 + 0.5 * lax.erf(pre * (0.5**0.5))
        ra[:, cols] = (pre * below).astype(BF)
        rs[:, cols] = (below + pre * (jnp.exp(-0.5 * pre * pre) * 0.3989422804014327)).astype(BF)

    if remote:
        gather.close()
        keep_w.wait()

    @pl.loop(0, 6)
    def _(n):
        cols = aligned(n * step, step, 128)
        down[cols, :] = tn(ra[:, cols], grad_mlp[...]).astype(BF)

    if remote:
        for j in range(job_down):
            reduce.ready(j)
        reduce.to_x(0)
        reduce.to_x(1)
    else:
        put_down = copy_in(down, r["down_o"], sems.at[4])
    load_down.wait()

    @pl.loop(0, 6)
    def _(n):
        cols = aligned(n * step, step, 128)
        rs[:, cols] = (nt(grad_mlp[...], wd[cols, :]) * rs[:, cols].astype(F32)).astype(BF)

    for n in range(3):
        cols = slice(n * width, (n + 1) * width)
        wide[:, cols] = nt(rs[...], wu[cols, :])

    tick()

    @pl.loop(0, parts)
    def _(h):
        cols = aligned(h * part, part, 128)
        wu[:, cols] = tn(normed_two[...], rs[:, cols]).astype(BF)

    if remote:
        for j in range(job_down, job_down + job_up):
            reduce.ready(j)
    else:
        put_up = copy_in(wu, r["up_o"], sems.at[5])

    blocks = [copy_in(w_all.at[columns : columns + features], rs.at[0:features, 0:features], sems.at[6])]
    for n in range(3):
        blocks.append(
            copy_in(
                w_all.at[n * features : (n + 1) * features],
                rs.at[0:features, (n + 1) * features : (n + 2) * features],
                sems.at[7 + n],
            )
        )

    vec[0] = jnp.zeros_like(vec[0])

    @pl.loop(0, owned)
    def _(i):
        rows = rows_of(i)
        rows_f = picked[rows, :].astype(F32)
        unit, scale = standardise(rows_f + attn[rows, :])
        grad = wide[rows, :]
        vec[0, 2:3, :] += jnp.sum(grad * unit, axis=0, keepdims=True)
        vec[0, 3:4, :] += jnp.sum(grad, axis=0, keepdims=True)
        wide[rows, :] = norm_pull(grad, unit, scale, gain_two)

    for n in range(3):
        cols = slice(n * width, (n + 1) * width)
        attn[:, cols] += nn(ra[...], wd[:, cols])

    reload = copy_in(saved_o, ra, sems.at[3])
    tick()

    @pl.loop(0, owned)
    def _(i):
        rows = rows_of(i)
        rows_f = picked[rows, :].astype(F32)
        gate, valid = row_gate(rows_f, w_router, counts[i])
        grads = picked_grad[rows, :].astype(F32)
        logit = valid * gate * (1.0 - gate) * jnp.sum(grads * attn[rows, :], axis=-1, keepdims=True)
        logits[rows, :] = jnp.broadcast_to(logit, (capacity, 128))
        vec[0, 4:5, :] += jnp.sum(logit * rows_f, axis=0, keepdims=True)
        grad_mlp[rows, :] = (gate * valid * grads + wide[rows, :]).astype(BF)

    wd[columns : columns + features, :] = tn(mixed[...], grad_mlp[...]).astype(BF)
    if remote:
        reduce.ready(job_down + job_up)
    blocks[0].wait()
    normed_two[...] = nt(grad_mlp[...], rs[0:features, 0:features]).astype(BF)
    tick()
    reload.wait()

    def attend_back(first, last):
        @pl.loop(first, last)
        def _(i):
            rows = rows_of(i)
            for pair in range(pairs):
                tiles, swapped, low, zero, heads = pair_tiles(proj, rows, pair)
                lanes = slice(2 * HEAD_DIM * pair, 2 * HEAD_DIM * (pair + 1))
                grads = normed_two[rows, lanes]
                halves = (jnp.where(low, grads, zero), jnp.where(low, zero, grads))
                found = []
                for h, (key_tile, query_tile) in enumerate(heads):
                    scores = head_scores(key_tile, query_tile, low, counts[i])
                    probs = jnp.exp(scores - totals[i, 2 * pair + h : 2 * pair + h + 1, :])
                    grad_probs = nt(tiles[1 + h], halves[h])
                    shift = jnp.sum(probs * grad_probs, axis=0, keepdims=True)
                    grad_scores = (probs * (grad_probs - shift)).astype(BF)
                    grad_value = nn(probs.astype(BF), grads)
                    scale = HEAD_DIM ** (-0.5)
                    grad_query = tn(grad_scores, swapped[2 * h]) * scale
                    grad_key = nn(grad_scores, swapped[h]) * scale
                    found.append((grad_query, grad_key, grad_value))
                (query_a, key_a, value_a), (query_b, key_b, value_b) = found
                proj[rows, pair_lanes(pair, 0)] = jnp.where(low, query_a, key_a).astype(BF)
                proj[rows, pair_lanes(pair, 1)] = jnp.where(low, value_a, query_b).astype(BF)
                proj[rows, pair_lanes(pair, 2)] = jnp.where(low, key_b, value_b).astype(BF)

    cuts = [0, owned // 3, (2 * owned) // 3, owned]
    for first, last in zip(cuts[:-1], cuts[1:]):
        attend_back(first, last)
        tick()

    for n in range(3):
        cols = slice(n * features, (n + 1) * features)
        wd[cols, :] = tn(proj[:, cols], normed_one[...]).astype(BF)
    if remote:
        for j in range(job_down + job_up + 1, reduce.jobs):
            reduce.ready(j)
        tick()
    else:
        put_qkv = copy_in(wd, r["qkv_out_o"], sems.at[0])

    for n in range(3):
        blocks[1 + n].wait()
    token_copy(0, 0).start()

    @pl.loop(0, owned)
    def _(i):
        slot = lax.rem(i, 2)

        @pl.when(i + 1 < owned)
        def _():
            token_copy(i + 1, 1 - slot).start()

        rows = rows_of(i)
        gate, valid = row_gate(picked[rows, :].astype(F32), w_router, counts[i])
        table = slot_table(slot_row(i), length)
        upper, lower = split_low(gate * valid * attn[rows, :])
        token_copy(i, slot).wait()

        @pl.when(i >= 2)
        def _():
            result_copy(i - 2, slot).wait()

        res[slot] = (tok[slot].astype(F32) + (nn(table, upper) + nn(table, lower))).astype(BF)
        result_copy(i, slot).start()

    tick()

    for n in range(3):
        cols = slice(n * width, (n + 1) * width)
        total = nn(proj[:, 0:features], rs[0:features, features + n * width : features + (n + 1) * width])
        for k in range(1, 3):
            base = (k + 1) * features + n * width
            total += nn(proj[:, k * features : (k + 1) * features], rs[0:features, base : base + width])
        attn[:, cols] = total

    cot_copy(0, 0).start()

    @pl.loop(0, owned)
    def _(i):
        slot = lax.rem(i, 2)

        @pl.when(i + 1 < owned)
        def _():
            cot_copy(i + 1, 1 - slot).start()

        rows = rows_of(i)
        rows_f = picked[rows, :].astype(F32)
        unit, scale = standardise(rows_f)
        grad = attn[rows, :]
        vec[0, 0:1, :] += jnp.sum(grad * unit, axis=0, keepdims=True)
        vec[0, 1:2, :] += jnp.sum(grad, axis=0, keepdims=True)
        back = norm_pull(grad, unit, scale, gain_one)
        total = back + wide[rows, :] + logits[rows, 0:1] * w_router
        table = slot_table(slot_row(i), length)
        upper, lower = split_low(total)
        cot_copy(i, slot).wait()

        @pl.when(i >= 2)
        def _():
            gtok_copy(i - 2, slot).wait()

        gtok[slot] = cot[slot].astype(F32) + (nn(table, upper) + nn(table, lower))
        gtok_copy(i, slot).start()

    if remote:
        stages = sum_vectors(place, vec, r["vec_in"], (r["vec_send"], r["vec_recv"]), reduce.sent)
        while ticks[0] < reduce.jobs + 4:
            if stages:
                stages.pop(0)()
            tick()
        while stages:
            stages.pop(0)()
        vec_o[...] = vec[vec.shape[0] - 1]
    else:
        vec_o[...] = vec[0]

    for i in range(max(owned - 2, 0), owned):
        result_copy(i, i % 2).wait()
        gtok_copy(i, i % 2).wait()
    if remote:
        reduce.close()
    else:
        put_down.wait()
        put_up.wait()
        put_qkv.wait()


def fused(
    parts, outer, tokens, slot_ids, counts, weights, w_up, w_down,
    gain_one, bias_one, gain_two, bias_two, w_router, cotangent,
):
    owned, length, features = tokens.shape
    capacity = slot_ids.shape[1]
    rows = owned * capacity
    hidden = w_up.shape[1]
    remote = outer > 0
    columns = weights[0].shape[0] * parts if remote else weights[0].shape[0] - features
    heads = columns // (3 * HEAD_DIM)
    vectors = jnp.stack([gain_one, bias_one, gain_two, bias_two, w_router])
    S = jax.ShapeDtypeStruct
    inside = pl.BlockSpec(memory_space=pltpu.VMEM)
    outside = pl.BlockSpec(memory_space=pltpu.HBM)
    scalars = pl.BlockSpec(memory_space=pltpu.SMEM)
    V = pltpu.VMEM
    D = pltpu.SemaphoreType.DMA
    ins = {
        "slots": (slot_ids, inside), "counts": (counts, scalars), "vectors": (vectors, inside),
        "tokens": (tokens, outside), "cotangent": (cotangent, outside),
        "w_up": (w_up, outside), "w_down": (w_down, outside),
    }
    outs = {
        "result_o": (S((owned, length, features), BF), outside),
        "grad_tokens_o": (S((owned, length, features), F32), outside),
        "vec_o": (S((8, features), F32), inside),
        "saved_o": (S((rows, columns + features), BF), outside),
    }
    steps = 3
    if remote:
        steps = 3 + outer.bit_length() - 1
    scratch = {
        "wu": V((features, hidden), BF), "wd": V((hidden, features), BF), "ra": V((rows, hidden), BF),
        "rs": V((rows, hidden), BF), "down": V((hidden, features), BF),
        "normed_two": V((rows, features), BF), "grad_mlp": V((rows, features), BF),
        "mixed": V((rows, features), BF), "attn": V((rows, features), F32), "wide": V((rows, features), F32),
        "picked": V((rows, features), BF), "picked_grad": V((rows, features), BF),
        "totals": V((owned, heads, capacity), F32), "logits": V((rows, 128), F32),
        "tok": V((2, length, features), BF), "cot": V((2, length, features), BF),
        "res": V((2, length, features), BF), "gtok": V((2, length, features), F32),
        "vec": V((steps + 1, 8, features), F32),
        "sems": D((10,)), "tok_sems": D((2,)), "cot_sems": D((2,)), "res_sems": D((2,)), "gtok_sems": D((2,)),
    }
    if remote:
        ins["w_qkv_t"] = (weights[0], outside)
        ins["w_out"] = (weights[1], outside)
        outs["w_saved_o"] = (S((columns + features, features), BF), outside)
        total = (columns + features + 2 * hidden) // parts
        jobs = total // JOB_ROWS
        outs["grads_o"] = (S((total, features), BF), outside)
        half = features // 2
        scratch.update({
            "from_core": V((jobs, 2, JOB_ROWS, features), BF), "from_x": V((jobs, JOB_ROWS, features), BF),
            "from_y": V((jobs, JOB_ROWS, half), BF),
            "from_z": V((jobs, outer - 1, JOB_ROWS // outer, half), BF),
            "vec_in": V((steps, 8, features), F32),
            "local_sems": D((2,)), "kept_sems": D((jobs,)),
        })
        for name, shape in (
            ("ag", (18,)), ("core", (jobs, 2)), ("x", (jobs,)), ("y", (jobs,)), ("z", (jobs, outer - 1)),
            ("az", (jobs, outer - 1)), ("ay", (jobs, outer)), ("vec", (steps,)),
        ):
            scratch[name + "_send"] = D(shape)
            scratch[name + "_recv"] = D(shape)
    else:
        ins["w_all"] = (weights[0], outside)
        outs["down_o"] = (S((hidden, features), BF), outside)
        outs["up_o"] = (S((features, hidden), BF), outside)
        outs["qkv_out_o"] = (S((columns + features, features), BF), outside)
    names = list(ins) + list(outs) + list(scratch)
    found = pl.pallas_call(
        functools.partial(fused_kernel, owned, length, capacity, parts, outer, names),
        out_shape=[v[0] for v in outs.values()],
        in_specs=[v[1] for v in ins.values()],
        out_specs=[v[1] for v in outs.values()],
        scratch_shapes=list(scratch.values()),
        compiler_params=pltpu.CompilerParams(
            vmem_limit_bytes=63 << 20,
            has_side_effects=remote,
            collective_id=0 if remote else None,
        ),
    )(*[v[0] for v in ins.values()])
    return dict(zip(outs, found))


def shards(
    images,
    tokens,
    slot_ids,
    counts,
    w_qkv,
    w_out,
    w_up,
    w_down,
    gain_one,
    bias_one,
    gain_two,
    bias_two,
    w_router,
    cotangent,
):
    features = tokens.shape[2]
    hidden = w_up.shape[1]
    parts = lax.axis_size("head")
    me = lax.axis_index("head")
    small = (gain_one, bias_one, gain_two, bias_two, w_router, cotangent)
    outer = images // 2 if images == 8 and parts == 4 else 0
    if outer:
        found = fused(
            parts, outer, tokens, slot_ids, counts, (w_qkv.T, w_out), w_up, w_down, *small
        )
        grads = found["grads_o"]
        part, rows = hidden // parts, w_out.shape[0]
        down = grads[:part].astype(F32)
        up = grads[part : part + features].astype(F32)
        out = grads[part + features : part + features + rows].astype(F32)
        qkv = grads[part + features + rows :].astype(F32).T
        vectors = found["vec_o"]
    else:
        w_all = jnp.concatenate(
            [
                lax.all_gather(w_qkv.T, "head", axis=0, tiled=True),
                lax.all_gather(w_out, "head", axis=0, tiled=True),
            ]
        )
        found = fused(parts, outer, tokens, slot_ids, counts, (w_all,), w_up, w_down, *small)
        columns = w_all.shape[0] - features

        def reduced(matrix, axis=0):
            shard = lax.psum_scatter(matrix, "head", scatter_dimension=axis, tiled=True)
            piece = lax.psum_scatter(shard, "img", scatter_dimension=0, tiled=True)
            return lax.all_gather(piece, "img", axis=0, tiled=True).astype(F32)

        both = found["qkv_out_o"]
        down, up = reduced(found["down_o"]), reduced(found["up_o"], 1)
        out, qkv = reduced(both[columns:]), reduced(both[:columns]).T
        vectors = lax.psum(found["vec_o"], ("img", "head"))
    vectors = lax.dynamic_slice_in_dim(
        vectors, me * (features // parts), features // parts, axis=1
    )
    return (
        found["result_o"],
        found["grad_tokens_o"],
        qkv,
        out,
        up,
        down,
        vectors[0],
        vectors[1],
        vectors[2],
        vectors[3],
        vectors[4],
    )


def solution(mesh):
    return jax.shard_map(
        functools.partial(shards, mesh.shape["img"]),
        mesh=mesh,
        in_specs=(
            P(("img", "head"), None, None),
            P(("img", "head"), None),
            P(("img", "head")),
            P(None, "head"),
            P("head", None),
            P(),
            P(),
            P(),
            P(),
            P(),
            P(),
            P(),
            P(("img", "head"), None, None),
        ),
        out_specs=(
            P(("img", "head"), None, None),
            P(("img", "head"), None, None),
            P(None, "head"),
            P("head", None),
            P(None, "head"),
            P("head", None),
            P("head"),
            P("head"),
            P("head"),
            P("head"),
            P("head"),
        ),
        check_vma=False,
    )
```

```python
import functools

import jax
import jax.numpy as jnp
from jax import lax
from jax.experimental import pallas as pl
from jax.experimental.pallas import tpu as pltpu
from jax.sharding import PartitionSpec as P

HEAD_DIM = 64
EPS = 1e-06
BF = jnp.bfloat16
F32 = jnp.float32


def nn(a, b):
    return lax.dot_general(a, b, (((1,), (0,)), ((), ())), preferred_element_type=F32)


def nt(a, b):
    return lax.dot_general(a, b, (((1,), (1,)), ((), ())), preferred_element_type=F32)


def tn(a, b):
    return lax.dot_general(a, b, (((0,), (0,)), ((), ())), preferred_element_type=F32)


def standardise(values):
    average = jnp.mean(values, axis=-1, keepdims=True)
    centred = values - average
    variance = jnp.mean(centred * centred, axis=-1, keepdims=True)
    scale = lax.rsqrt(variance + EPS)
    return centred * scale, scale


def norm_pull(grad, unit, scale, gain):
    inner = grad * gain
    first = jnp.mean(inner, axis=-1, keepdims=True)
    second = jnp.mean(inner * unit, axis=-1, keepdims=True)
    return scale * (inner - first - unit * second)


def split_low(values):
    upper = values.astype(BF)
    return upper, (values - upper.astype(F32)).astype(BF)


def slot_table(slots, length):
    capacity = slots.shape[1]
    return (lax.broadcasted_iota(jnp.int32, (length, capacity), 0) == slots).astype(BF)


def row_gate(picked, w_router, count):
    gate = jax.nn.sigmoid(jnp.sum(picked * w_router, axis=-1, keepdims=True))
    valid = (lax.broadcasted_iota(jnp.int32, gate.shape, 0) < count).astype(F32)
    return gate, valid


def lane_low(shape):
    return lax.broadcasted_iota(jnp.int32, shape, 1) < HEAD_DIM


def head_scores(key_tile, query_tile, low, count):
    scores = nt(key_tile, query_tile)
    seen = lax.broadcasted_iota(jnp.int32, scores.shape, 0) < count
    return jnp.where(seen, scores, -1e30)


def swap_halves(tile):
    return pltpu.roll(tile.astype(F32), HEAD_DIM, 1).astype(BF)


def pair_lanes(pair, t):
    return pl.ds(pl.multiple_of((3 * pair + t) * 2 * HEAD_DIM, 128), 2 * HEAD_DIM)


def pair_tiles(proj, rows, pair):
    tiles = [proj[rows, pair_lanes(pair, t)] for t in range(3)]
    low = lane_low(tiles[0].shape)
    zero = jnp.zeros_like(tiles[0])
    swapped = [swap_halves(tile) for tile in tiles]
    scale = HEAD_DIM ** (-0.5)
    query_a = jnp.where(low, tiles[0], zero) * jnp.asarray(scale, BF)
    query_b = jnp.where(low, swapped[1], zero) * jnp.asarray(scale, BF)
    return tiles, swapped, low, zero, ((swapped[0], query_a), (tiles[2], query_b))

MESH_ID = pl.DeviceIdType.MESH
AG_ROWS = 96


def copy_in(source, target, sem):
    copy = pltpu.make_async_copy(source, target, sem)
    copy.start()
    return copy


def aligned(start, size, unit=16):
    return pl.ds(pl.multiple_of(start, unit), size)


class Place:
    def __init__(self, outer):
        self.head = lax.axis_index("head")
        self.img = lax.axis_index("img")
        self.outer = outer
        self.x, self.c = self.head // 2, self.head % 2
        self.z, self.y = self.img // 2, self.img % 2
        self.own = self.head
        self.across = 2 * (1 - self.x) + self.c
        self.core_at = (self.img, 2 * self.x + 1 - self.c)
        self.x_at = (self.img, self.across)
        self.y_at = (2 * self.z + 1 - self.y, self.head)
        self.z_at = []
        self.z_of = []
        for k in range(1, outer):
            other = lax.rem(self.z + k, outer)
            self.z_of.append(other)
            self.z_at.append((2 * other + self.y, self.head))


def remote(source, target, sems, index, device):
    return pltpu.make_async_remote_copy(
        src_ref=source,
        dst_ref=target,
        send_sem=sems[0].at[index],
        recv_sem=sems[1].at[index],
        device_id=device,
        device_id_type=MESH_ID,
    )


def send(source, target, sems, index, device):
    copy = remote(source, target, sems, index, device)
    copy.start()
    return copy


class Gather:
    def __init__(self, place, whole, w_qkv_t, w_out, sems, local_sems):
        self.p, self.whole, self.sems = place, whole, sems
        self.w = (w_qkv_t, w_out)
        self.sizes = (w_qkv_t.shape[0], w_out.shape[0])
        self.columns = 4 * self.sizes[0]
        self.local_sems = local_sems
        self.split = (self.sizes[0] // 2) // AG_ROWS
        self.steps = self.split + 1

    def part(self, shard, kind, first=0, size=None):
        base = shard * self.sizes[kind] + (self.columns if kind else 0) + first
        return self.whole.at[aligned(base, size or self.sizes[kind])]

    def first_row(self, side, t):
        return side * AG_ROWS if t == self.split else (self.split * side + t) * AG_ROWS

    def piece(self, shard, side, t):
        return self.part(shard, int(t == self.split), self.first_row(side, t), AG_ROWS)

    def source(self, side, t):
        return self.w[int(t == self.split)].at[aligned(self.first_row(side, t), AG_ROWS)]

    def local(self, k):
        return pltpu.make_async_copy(self.w[k], self.part(self.p.own, k), self.local_sems.at[k])

    def core(self, k):
        return remote(self.w[k], self.part(self.p.own, k), self.sems, k, self.p.core_at)

    def over_x(self, t):
        p = self.p
        return remote(self.source(p.y, t), self.piece(p.own, p.y, t), self.sems, 2 + t, p.x_at)

    def over_y(self, t):
        p = self.p
        block = self.piece(p.across, p.y, t)
        return remote(block, block, self.sems, 2 + self.steps + t, p.y_at)

    def passed(self, t):
        p, n = self.p, self.steps
        side = p.y if t < n else 1 - p.y
        block = self.piece(p.across, side, t % n)
        return remote(block, block, self.sems, 2 + 2 * n + t, p.core_at)

    def begin(self):
        for k in range(2):
            self.local(k).start()
            self.core(k).start()
        for t in range(self.steps):
            self.over_x(t).start()

    def own_half(self):
        for k in range(2):
            self.local(k).wait()
            self.core(k).wait_recv()

    def forward_x(self, t):
        self.over_x(t).wait_recv()
        self.over_y(t).start()
        self.passed(t).start()

    def forward_y(self, t):
        self.over_y(t).wait_recv()
        self.passed(self.steps + t).start()

    def other_half(self, steps):
        for t in steps:
            self.passed(t).wait_recv()
            self.passed(self.steps + t).wait_recv()

    def close(self):
        for k in range(2):
            self.core(k).wait_send()
        for t in range(self.steps):
            self.over_x(t).wait_send()
            self.over_y(t).wait_send()
        for t in range(2 * self.steps):
            self.passed(t).wait_send()


def add_into(block, *others):
    rows = 64 if block.shape[0] % 64 == 0 else 16

    @pl.loop(0, block.shape[0] // rows)
    def _(n):
        part = aligned(n * rows, rows)
        total = block[part, :].astype(F32)
        for other in others:
            total += other[part, :].astype(F32)
        block[part, :] = total.astype(BF)


class Reduce:
    def __init__(self, place, jobs, out, buffers, sems, local_sem):
        self.p, self.out = place, out
        self.blocks = [job[0] for job in jobs]
        self.rows = [job[1] for job in jobs]
        self.target = [job[2] for job in jobs]
        self.base = [sum(self.rows[:j]) for j in range(len(jobs))]
        self.from_core, self.from_x, self.from_y, self.from_z = buffers
        self.core_sems, self.x_sems, self.y_sems, self.z_sems, self.az_sems, self.ay_sems = sems
        self.local_sem = local_sem
        self.jobs = len(jobs)
        self.sent = []
        self.kept = []
        self.core, self.over_x, self.over_y = {}, {}, {}
        self.over_z, self.all_z, self.all_y = {}, {}, {}
        self.half = out.shape[1] // 2
        self.mine = aligned(place.y * self.half, self.half, 128)
        self.theirs = aligned((1 - place.y) * self.half, self.half, 128)

    def span(self, j):
        return slice(self.base[j], self.base[j] + self.rows[j])

    def ready(self, j):
        p = self.p
        shards = [(1 - p.x), p.x]
        self.core[j] = [
            send(
                self.blocks[j](2 * xx + 1 - p.c), self.from_core.at[xx, self.span(j)],
                self.core_sems, (j, n), p.core_at,
            )
            for n, xx in enumerate(shards)
        ]
        self.sent += self.core[j]

    def to_x(self, j):
        p = self.p
        self.core[j][0].wait_recv()
        block = self.blocks[j](p.across)
        add_into(block, self.from_core.at[1 - p.x, self.span(j)])
        self.over_x[j] = send(block, self.from_x.at[self.span(j)], self.x_sems, j, p.x_at)
        self.sent.append(self.over_x[j])

    def to_y(self, j):
        p = self.p
        self.core[j][1].wait_recv()
        self.over_x[j].wait_recv()
        block = self.blocks[j](p.own)
        add_into(block, self.from_core.at[p.x, self.span(j)], self.from_x.at[self.span(j)])
        self.over_y[j] = send(
            block.at[:, self.theirs], self.from_y.at[self.span(j)], self.y_sems, j, p.y_at
        )
        self.sent.append(self.over_y[j])

    def quarters(self, j):
        size = self.rows[j] // self.p.outer
        base = self.base[j] // self.p.outer
        return size, slice(base, base + size)

    def to_z(self, j):
        p = self.p
        self.over_y[j].wait_recv()
        block = self.blocks[j](p.own).at[:, self.mine]
        add_into(block, self.from_y.at[self.span(j)])
        size, span = self.quarters(j)
        self.over_z[j] = [
            send(
                block.at[aligned(size * p.z_of[k], size)], self.from_z.at[k, span],
                self.z_sems, (j, k), p.z_at[k],
            )
            for k in range(p.outer - 1)
        ]
        self.sent += self.over_z[j]

    def place_of(self, j, z, lanes):
        size, _ = self.quarters(j)
        return self.out.at[aligned(self.target[j] + size * z, size), lanes]

    def spread(self, j):
        p = self.p
        for copy in self.over_z[j]:
            copy.wait_recv()
        size, span = self.quarters(j)
        piece = self.blocks[j](p.own).at[aligned(size * p.z, size), self.mine]
        add_into(piece, *[self.from_z.at[k, span] for k in range(p.outer - 1)])
        target = self.place_of(j, p.z, self.mine)
        self.kept.append(copy_in(piece, target, self.local_sem.at[j]))
        self.all_z[j] = [
            send(piece, target, self.az_sems, (j, k), p.z_at[k]) for k in range(p.outer - 1)
        ]
        self.all_y[j] = [send(piece, target, self.ay_sems, (j, 0), p.y_at)]
        self.sent += self.all_z[j] + self.all_y[j]

    def across_y(self, j):
        p = self.p
        for k in range(p.outer - 1):
            self.all_z[j][k].wait_recv()
            z = lax.rem(p.z + p.outer - 1 - k, p.outer)
            block = self.place_of(j, z, self.mine)
            copy = send(block, block, self.ay_sems, (j, k + 1), p.y_at)
            self.all_y[j].append(copy)
            self.sent.append(copy)

    def finish(self, j):
        for copy in self.all_y[j]:
            copy.wait_recv()

    def feed(self, last):
        for j in range(min(last + 1, self.jobs)):
            if j in self.core and j not in self.over_x:
                self.to_x(j)

    def tick(self, t):
        for lag, step in enumerate((self.to_y, self.to_z, self.spread, self.across_y, self.finish)):
            if 0 <= t - lag < self.jobs:
                step(t - lag)

    def close(self):
        for copy in self.sent:
            copy.wait_send()
        for copy in self.kept:
            copy.wait()


def sum_vectors(place, vec, inbox, sems, sent):
    p = place
    partners = [p.core_at, p.x_at, p.y_at]
    bit = 1
    while bit < p.outer:
        low = lax.rem(p.z // bit, 2)
        partners.append((2 * (p.z + bit - 2 * bit * low) + p.y, p.head))
        bit *= 2
    count = len(partners)
    copies = []

    def stage(n):
        if n:
            copies[n - 1].wait_recv()
            vec[n] = vec[n - 1] + inbox[n - 1]
        if n < count:
            copies.append(send(vec.at[n], inbox.at[n], sems, n, partners[n]))
            sent.append(copies[n])

    return [functools.partial(stage, n) for n in range(count + 1)]


def fused_kernel(owned, length, capacity, parts, outer, names, *refs):
    r = dict(zip(names, refs))
    remote = outer > 0
    slots, counts = r["slots"], r["counts"]
    gain_one, bias_one, gain_two, bias_two, w_router = (
        r[k][...][None, :] for k in ("gain_one", "bias_one", "gain_two", "bias_two", "w_router")
    )
    tokens, cotangent = r["tokens"], r["cotangent"]
    wu, wd, ra, rs, down = r["wu"], r["wd"], r["ra"], r["rs"], r["down"]
    normed_two, grad_mlp, mixed, attn, wide = (
        r[k] for k in ("normed_two", "grad_mlp", "mixed", "attn", "wide")
    )
    picked, picked_grad, totals, logits = (r[k] for k in ("picked", "picked_grad", "totals", "logits"))
    tok, cot, res, gtok = (r[k] for k in ("tok", "cot", "res", "gtok"))
    sems, tok_sems, cot_sems, res_sems, gtok_sems = (
        r[k] for k in ("sems", "tok_sems", "cot_sems", "res_sems", "gtok_sems")
    )
    result_o, grad_tokens_o, saved_o, vec_o = (
        r[k] for k in ("result_o", "grad_tokens_o", "saved_o", "vec_o")
    )
    vec = r["vec"]
    features, hidden = wu.shape
    columns = wd.shape[0] - features
    pairs = columns // (6 * HEAD_DIM)
    proj = ra.at[:, 0:columns]
    normed_one = ra.at[:, columns : columns + features]
    width = features // 3
    part = hidden // parts
    rows_all = owned * capacity
    piece = features // 3

    def rows_of(i):
        return aligned(i * capacity, capacity)

    def slot_row(i):
        return slots[pl.ds(i, 1), :]

    def token_copy(i, slot):
        return pltpu.make_async_copy(tokens.at[i], tok.at[slot], tok_sems.at[slot])

    def cot_copy(i, slot):
        return pltpu.make_async_copy(cotangent.at[i], cot.at[slot], cot_sems.at[slot])

    def result_copy(i, slot):
        return pltpu.make_async_copy(res.at[slot], result_o.at[i], res_sems.at[slot])

    def gtok_copy(i, slot):
        return pltpu.make_async_copy(gtok.at[slot], grad_tokens_o.at[i], gtok_sems.at[slot])

    token_copy(0, 0).start()
    cot_copy(0, 0).start()
    reduce = None
    if remote:
        place = Place(outer)
        barrier = pltpu.get_barrier_semaphore()
        partners = [place.core_at, place.x_at, place.y_at, *place.z_at]
        for partner in partners:
            pl.semaphore_signal(barrier, inc=1, device_id=partner, device_id_type=MESH_ID)
        pl.semaphore_wait(barrier, len(partners))
        gather = Gather(
            place, down, r["w_qkv_t"], r["w_out"], (r["ag_send"], r["ag_recv"]), r["local_sems"]
        )
        gather.begin()
        w_all = r["w_saved_o"]
        half_order = (place.x, 1 - place.x)

        def rows_block(ref, base, step, rows):
            return lambda s: ref.at[aligned(s * step + base, rows)]

        def lanes_block(ref, base, rows):
            return lambda s: ref.at[base : base + rows, aligned(s * part, part, 128)]

        def head_block(ref, q, rows):
            return lambda s: ref.at[aligned(s * share + lax.rem(q + s % 2, 3) * rows, rows)]

        share = columns // parts
        out_rows = features // parts
        jobs = [
            (rows_block(down, piece * k, part, piece), piece, piece * k) for k in range(part // piece)
        ]
        jobs += [
            (lanes_block(wu, features // 2 * k, features // 2), features // 2, part + features // 2 * k)
            for k in range(2)
        ]
        after = part + features
        jobs += [(rows_block(wd, columns, out_rows, out_rows), out_rows, after)]
        after += out_rows
        jobs += [
            (head_block(wd, q, share // 3), share // 3, after + lax.rem(q + place.c, 3) * (share // 3))
            for q in range(3)
        ]
        reduce = Reduce(
            place, jobs, r["grads_o"], [r[k] for k in ("from_core", "from_x", "from_y", "from_z")],
            [(r[k + "_send"], r[k + "_recv"]) for k in ("core", "x", "y", "z", "az", "ay")],
            r["kept_sems"],
        )
        job_down, job_up = part // piece, 2
    else:
        job_down, job_up = part // piece, 2
        w_all = r["w_all"]
        load_w = copy_in(w_all, down, sems.at[0])
        half_order = (0, 1)
    load_up = copy_in(r["w_up"], wu, sems.at[1])
    load_down = copy_in(r["w_down"], wd, sems.at[2])
    ticks = [0]

    def tick():
        if remote:
            reduce.tick(ticks[0])
            ticks[0] += 1

    @pl.loop(0, owned)
    def _(i):
        slot = lax.rem(i, 2)

        @pl.when(i + 1 < owned)
        def _():
            token_copy(i + 1, 1 - slot).start()
            cot_copy(i + 1, 1 - slot).start()

        rows = rows_of(i)
        table = slot_table(slot_row(i), length)
        token_copy(i, slot).wait()
        rows_f = tn(table, tok[slot])
        picked[rows, :] = rows_f.astype(BF)
        unit, _ = standardise(rows_f)
        normed_one[rows, :] = (unit * gain_one + bias_one).astype(BF)
        gate, valid = row_gate(rows_f, w_router, counts[i])
        cot_copy(i, slot).wait()
        grads = tn(table, cot[slot])
        picked_grad[rows, :] = grads.astype(BF)
        grad_mlp[rows, :] = (gate * valid * grads).astype(BF)

    def project(half):
        base = pl.multiple_of(half * (columns // 2), 128)
        size = rows_all // 3

        @pl.loop(0, 3)
        def _(n):
            rows = aligned(n * size, size)
            proj[rows, pl.ds(base, columns // 2)] = nt(
                normed_one[rows, :], down[pl.ds(base, columns // 2), :]
            ).astype(BF)

    def attend(half, i):
        rows = rows_of(i)
        for p in range(pairs // 2):
            pair = half * (pairs // 2) + p
            tiles, swapped, low, zero, heads = pair_tiles(proj, rows, pair)
            outs = []
            for h, (key_tile, query_tile) in enumerate(heads):
                scores = head_scores(key_tile, query_tile, low, counts[i])
                highest = jnp.max(scores, axis=0, keepdims=True)
                terms = jnp.exp(scores - highest)
                total = jnp.sum(terms, axis=0, keepdims=True)
                probs = (terms * (1.0 / total)).astype(BF)
                totals[i, pl.ds(2 * pair + h, 1), :] = highest + jnp.log(total)
                outs.append(tn(probs, tiles[1 + h]))
            mixed[rows, aligned(2 * HEAD_DIM * pair, 2 * HEAD_DIM, 128)] = jnp.where(
                low, outs[0], outs[1]
            ).astype(BF)

    if remote:
        gather.forward_x(0)
        gather.own_half()
    else:
        load_w.wait()

    @pl.loop(0, 2)
    def _(turn):
        if remote:
            half = place.x + turn - 2 * place.x * turn

            @pl.when(turn == 1)
            def _():
                gather.forward_y(2)
                gather.other_half(range(gather.split))
        else:
            half = turn
        project(half)

        @pl.loop(0, owned)
        def _(i):
            if remote:
                for at, steps in ((0, ((0, 1),)), (2, ((0, 2), (1, 0))), (4, ((1, 1),))):

                    @pl.when((turn == 0) & (i == at))
                    def _(steps=steps):
                        for kind, t in steps:
                            (gather.forward_y if kind else gather.forward_x)(t)

                @pl.when((turn == 1) & (i == 0))
                def _():
                    gather.forward_x(3)

                @pl.when((turn == 1) & (i == 3))
                def _():
                    gather.forward_y(3)

            attend(half, i)

    if remote:
        gather.other_half((gather.split,))
        keep_w = copy_in(down, w_all, sems.at[0])
    save = copy_in(ra, saved_o, sems.at[3])

    @pl.loop(0, 3)
    def _(n):
        cols = aligned(n * width, width, 128)
        attn[:, cols] = nn(mixed[...], down[columns : columns + features, cols])

    @pl.loop(0, owned)
    def _(i):
        rows = rows_of(i)
        unit, _ = standardise(picked[rows, :].astype(F32) + attn[rows, :])
        normed_two[rows, :] = (unit * gain_two + bias_two).astype(BF)

    save.wait()
    load_up.wait()
    step = hidden // 6
    for k in range(part // piece):

        @pl.loop(0, parts)
        def _(h):
            cols = aligned(h * part + k * piece, piece, 128)
            pre = nn(normed_two[...], wu[:, cols])
            below = 0.5 + 0.5 * lax.erf(pre * (0.5**0.5))
            ra[:, cols] = (pre * below).astype(BF)
            rs[:, cols] = (below + pre * (jnp.exp(-0.5 * pre * pre) * 0.3989422804014327)).astype(BF)

        if remote and k == 0:
            gather.close()
            keep_w.wait()
        if remote and k:
            reduce.feed(k - 1)

        @pl.loop(0, parts)
        def _(h):
            cols = aligned(h * part + k * piece, piece, 128)
            down[cols, :] = tn(ra[:, cols], grad_mlp[...]).astype(BF)

        if remote:
            reduce.ready(k)

    if not remote:
        put_down = copy_in(down, r["down_o"], sems.at[4])
    load_down.wait()

    @pl.loop(0, 6)
    def _(n):
        cols = aligned(n * step, step, 128)
        rs[:, cols] = (nt(grad_mlp[...], wd[cols, :]) * rs[:, cols].astype(F32)).astype(BF)

    if remote:
        reduce.feed(job_down - 1)

    @pl.loop(0, 3)
    def _(n):
        cols = aligned(n * width, width, 128)
        wide[:, cols] = nt(rs[...], wu[cols, :])

    tick()
    step_up = features // job_up
    for k in range(job_up):

        @pl.loop(0, parts)
        def _(h):
            cols = aligned(h * part, part, 128)
            rows = slice(k * step_up, (k + 1) * step_up)
            wu[rows, cols] = tn(normed_two[:, rows], rs[:, cols]).astype(BF)

        if remote:
            if k:
                reduce.feed(job_down + k - 1)
            reduce.ready(job_down + k)

    tick()
    if not remote:
        put_up = copy_in(wu, r["up_o"], sems.at[5])

    blocks = [copy_in(w_all.at[columns : columns + features], rs.at[0:features, 0:features], sems.at[6])]
    for n in range(3):
        blocks.append(
            copy_in(
                w_all.at[n * features : (n + 1) * features],
                rs.at[0:features, (n + 1) * features : (n + 2) * features],
                sems.at[7 + n],
            )
        )

    vec[0] = jnp.zeros_like(vec[0])

    @pl.loop(0, owned)
    def _(i):
        rows = rows_of(i)
        rows_f = picked[rows, :].astype(F32)
        unit, scale = standardise(rows_f + attn[rows, :])
        grad = wide[rows, :]
        vec[0, 2:3, :] += jnp.sum(grad * unit, axis=0, keepdims=True)
        vec[0, 3:4, :] += jnp.sum(grad, axis=0, keepdims=True)
        wide[rows, :] = norm_pull(grad, unit, scale, gain_two)

    @pl.loop(0, 3)
    def _(n):
        cols = aligned(n * width, width, 128)
        attn[:, cols] += nn(ra[...], wd[:, cols])

    reload = copy_in(saved_o, ra, sems.at[3])
    if remote:
        reduce.feed(job_down + job_up - 1)
    tick()

    @pl.loop(0, owned)
    def _(i):
        rows = rows_of(i)
        rows_f = picked[rows, :].astype(F32)
        gate, valid = row_gate(rows_f, w_router, counts[i])
        grads = picked_grad[rows, :].astype(F32)
        logit = valid * gate * (1.0 - gate) * jnp.sum(grads * attn[rows, :], axis=-1, keepdims=True)
        logits[rows, :] = jnp.broadcast_to(logit, (capacity, 128))
        vec[0, 4:5, :] += jnp.sum(logit * rows_f, axis=0, keepdims=True)
        grad_mlp[rows, :] = (gate * valid * grads + wide[rows, :]).astype(BF)

    @pl.loop(0, 3)
    def _(n):
        cols = aligned(n * width, width, 128)
        wd[columns : columns + features, cols] = tn(mixed[...], grad_mlp[:, cols]).astype(BF)

    if remote:
        reduce.ready(job_down + job_up)
    blocks[0].wait()
    @pl.loop(0, 3)
    def _(n):
        cols = aligned(n * width, width, 128)
        normed_two[:, cols] = nt(grad_mlp[...], rs[cols, 0:features]).astype(BF)

    tick()
    reload.wait()

    def attend_back(chosen, first, last):
        @pl.loop(first, last)
        def _(i):
            rows = rows_of(i)
            for pair in chosen:
                tiles, swapped, low, zero, heads = pair_tiles(proj, rows, pair)
                lanes = slice(2 * HEAD_DIM * pair, 2 * HEAD_DIM * (pair + 1))
                grads = normed_two[rows, lanes]
                halves = (jnp.where(low, grads, zero), jnp.where(low, zero, grads))
                found = []
                for h, (key_tile, query_tile) in enumerate(heads):
                    scores = head_scores(key_tile, query_tile, low, counts[i])
                    probs = jnp.exp(scores - totals[i, 2 * pair + h : 2 * pair + h + 1, :])
                    grad_probs = nt(tiles[1 + h], halves[h])
                    shift = jnp.sum(probs * grad_probs, axis=0, keepdims=True)
                    grad_scores = (probs * (grad_probs - shift)).astype(BF)
                    grad_value = nn(probs.astype(BF), grads)
                    scale = HEAD_DIM ** (-0.5)
                    grad_query = tn(grad_scores, swapped[2 * h]) * scale
                    grad_key = nn(grad_scores, swapped[h]) * scale
                    found.append((grad_query, grad_key, grad_value))
                (query_a, key_a, value_a), (query_b, key_b, value_b) = found
                proj[rows, pair_lanes(pair, 0)] = jnp.where(low, query_a, key_a).astype(BF)
                proj[rows, pair_lanes(pair, 1)] = jnp.where(low, value_a, query_b).astype(BF)
                proj[rows, pair_lanes(pair, 2)] = jnp.where(low, key_b, value_b).astype(BF)

    early = [p for p in range(pairs) if p % 3 != 1]
    late = [p for p in range(pairs) if p % 3 == 1]

    def grad_qkv(count, pair_at):
        @pl.loop(0, count)
        def _(n):
            cols = aligned(pair_at(n) * 6 * HEAD_DIM, 6 * HEAD_DIM, 128)
            wd[cols, :] = tn(proj[:, cols], normed_one[...]).astype(BF)

    if remote:
        reduce.feed(job_down + job_up)
    attend_back(early, 0, owned // 2)
    tick()
    attend_back(early, owned // 2, owned)
    grad_qkv(len(early), lambda n: n + (n + 1) // 2)
    first_qkv = job_down + job_up + 1 if remote else 0
    if remote:
        reduce.ready(first_qkv)
        reduce.ready(first_qkv + 1)
    tick()
    attend_back(late, 0, owned // 2)
    if remote:
        reduce.feed(first_qkv + 1)
    attend_back(late, owned // 2, owned)
    grad_qkv(len(late), lambda n: 3 * n + 1)
    if remote:
        reduce.ready(first_qkv + 2)
    else:
        put_qkv = copy_in(wd, r["qkv_out_o"], sems.at[0])

    for n in range(3):
        blocks[1 + n].wait()
    token_copy(0, 0).start()

    def put_results(first, last):
        @pl.loop(first, last)
        def _(i):
            slot = lax.rem(i, 2)

            @pl.when(i + 1 < owned)
            def _():
                token_copy(i + 1, 1 - slot).start()

            rows = rows_of(i)
            gate, valid = row_gate(picked[rows, :].astype(F32), w_router, counts[i])
            table = slot_table(slot_row(i), length)
            upper, lower = split_low(gate * valid * attn[rows, :])
            token_copy(i, slot).wait()

            @pl.when(i >= 2)
            def _():
                result_copy(i - 2, slot).wait()

            res[slot] = (tok[slot].astype(F32) + (nn(table, upper) + nn(table, lower))).astype(BF)
            result_copy(i, slot).start()

    put_results(0, owned // 2)
    if remote:
        reduce.feed(first_qkv + 2)
    tick()
    put_results(owned // 2, owned)

    @pl.loop(0, 3)
    def _(n):
        cols = aligned(n * width, width, 128)
        total = nn(proj[:, 0:features], rs[0:features, aligned(features + n * width, width, 128)])
        for k in range(1, 3):
            total += nn(
                proj[:, k * features : (k + 1) * features],
                rs[0:features, aligned((k + 1) * features + n * width, width, 128)],
            )
        attn[:, cols] = total

    tick()
    cot_copy(0, 0).start()

    @pl.loop(0, owned)
    def _(i):
        slot = lax.rem(i, 2)

        @pl.when(i + 1 < owned)
        def _():
            cot_copy(i + 1, 1 - slot).start()

        rows = rows_of(i)
        rows_f = picked[rows, :].astype(F32)
        unit, scale = standardise(rows_f)
        grad = attn[rows, :]
        vec[0, 0:1, :] += jnp.sum(grad * unit, axis=0, keepdims=True)
        vec[0, 1:2, :] += jnp.sum(grad, axis=0, keepdims=True)
        back = norm_pull(grad, unit, scale, gain_one)
        total = back + wide[rows, :] + logits[rows, 0:1] * w_router
        table = slot_table(slot_row(i), length)
        upper, lower = split_low(total)
        cot_copy(i, slot).wait()

        @pl.when(i >= 2)
        def _():
            gtok_copy(i - 2, slot).wait()

        gtok[slot] = cot[slot].astype(F32) + (nn(table, upper) + nn(table, lower))
        gtok_copy(i, slot).start()

    if remote:
        stages = sum_vectors(place, vec, r["vec_in"], (r["vec_send"], r["vec_recv"]), reduce.sent)
        while ticks[0] < reduce.jobs + 4:
            if stages:
                stages.pop(0)()
            tick()
        while stages:
            stages.pop(0)()
        vec_o[...] = vec[vec.shape[0] - 1]
    else:
        vec_o[...] = vec[0]

    for i in range(max(owned - 2, 0), owned):
        result_copy(i, i % 2).wait()
        gtok_copy(i, i % 2).wait()
    if remote:
        reduce.close()
    else:
        put_down.wait()
        put_up.wait()
        put_qkv.wait()


def finish_kernel(sizes, *refs):
    grads, result, grad_tokens = refs[:3]
    outs, result_o, grad_tokens_o = refs[3:7], refs[7], refs[8]
    narrow, wide, kept_rows, kept_grads, in_sems, out_sems, row_sems = refs[9:]
    rows_in = [copy_in(result, kept_rows, row_sems.at[0]), copy_in(grad_tokens, kept_grads, row_sems.at[1])]
    chunk = 192
    places = [(out, r) for out, size in zip(outs, sizes) for r in range(0, size, chunk)]
    loads, copies = [], []
    for n in range(len(places)):
        rows = slice(n * chunk, (n + 1) * chunk)
        loads.append(copy_in(grads.at[rows], narrow.at[rows], in_sems.at[n]))
    for n, (out, r) in enumerate(places):
        rows = slice(n * chunk, (n + 1) * chunk)
        loads[n].wait()
        wide[rows, :] = narrow[rows, :].astype(F32)
        copies.append(copy_in(wide.at[rows], out.at[r : r + chunk], out_sems.at[n]))
        if n == 0:
            rows_in[0].wait()
            copies.append(copy_in(kept_rows, result_o, row_sems.at[2]))
            rows_in[1].wait()
            copies.append(copy_in(kept_grads, grad_tokens_o, row_sems.at[3]))
    for copy in copies:
        copy.wait()


def finish(grads, sizes, result, grad_tokens):
    total, features = grads.shape
    outside = pl.BlockSpec(memory_space=pltpu.HBM)
    S = jax.ShapeDtypeStruct
    D = pltpu.SemaphoreType.DMA
    shapes = [S((size, features), F32) for size in sizes]
    shapes += [S(result.shape, result.dtype), S(grad_tokens.shape, grad_tokens.dtype)]
    return pl.pallas_call(
        functools.partial(finish_kernel, sizes),
        out_shape=shapes,
        in_specs=[outside] * 3,
        out_specs=[outside] * len(shapes),
        scratch_shapes=[
            pltpu.VMEM((total, features), BF), pltpu.VMEM((total, features), F32),
            pltpu.VMEM(result.shape, BF), pltpu.VMEM(grad_tokens.shape, F32),
            D((total // 192,)), D((total // 192,)), D((4,)),
        ],
        compiler_params=pltpu.CompilerParams(vmem_limit_bytes=60 << 20),
    )(grads, result, grad_tokens)


def fused(
    parts, outer, tokens, slot_ids, counts, weights, w_up, w_down,
    gain_one, bias_one, gain_two, bias_two, w_router, cotangent,
):
    owned, length, features = tokens.shape
    capacity = slot_ids.shape[1]
    rows = owned * capacity
    hidden = w_up.shape[1]
    remote = outer > 0
    columns = weights[0].shape[0] * parts if remote else weights[0].shape[0] - features
    heads = columns // (3 * HEAD_DIM)
    S = jax.ShapeDtypeStruct
    inside = pl.BlockSpec(memory_space=pltpu.VMEM)
    outside = pl.BlockSpec(memory_space=pltpu.HBM)
    scalars = pl.BlockSpec(memory_space=pltpu.SMEM)
    V = pltpu.VMEM
    D = pltpu.SemaphoreType.DMA
    ins = {
        "slots": (slot_ids, inside), "counts": (counts, scalars),
        "gain_one": (gain_one, inside), "bias_one": (bias_one, inside), "gain_two": (gain_two, inside),
        "bias_two": (bias_two, inside), "w_router": (w_router, inside),
        "tokens": (tokens, outside), "cotangent": (cotangent, outside),
        "w_up": (w_up, outside), "w_down": (w_down, outside),
    }
    outs = {
        "result_o": (S((owned, length, features), BF), outside),
        "grad_tokens_o": (S((owned, length, features), F32), outside),
        "vec_o": (S((8, features), F32), inside),
        "saved_o": (S((rows, columns + features), BF), outside),
    }
    steps = 3
    if remote:
        steps = 3 + outer.bit_length() - 1
    scratch = {
        "wu": V((features, hidden), BF), "wd": V((hidden, features), BF), "ra": V((rows, hidden), BF),
        "rs": V((rows, hidden), BF), "down": V((hidden, features), BF),
        "normed_two": V((rows, features), BF), "grad_mlp": V((rows, features), BF),
        "mixed": V((rows, features), BF), "attn": V((rows, features), F32), "wide": V((rows, features), F32),
        "picked": V((rows, features), BF), "picked_grad": V((rows, features), BF),
        "totals": V((owned, heads, capacity), F32), "logits": V((rows, 128), F32),
        "tok": V((2, length, features), BF), "cot": V((2, length, features), BF),
        "res": V((2, length, features), BF), "gtok": V((2, length, features), F32),
        "vec": V((steps + 1, 8, features), F32),
        "sems": D((10,)), "tok_sems": D((2,)), "cot_sems": D((2,)), "res_sems": D((2,)), "gtok_sems": D((2,)),
    }
    if remote:
        ins["w_qkv_t"] = (weights[0], outside)
        ins["w_out"] = (weights[1], outside)
        outs["w_saved_o"] = (S((columns + features, features), BF), outside)
        total = (columns + features + 2 * hidden) // parts
        jobs = 9
        outs["grads_o"] = (S((total, features), BF), outside)
        half = features // 2
        scratch.update({
            "from_core": V((2, total, features), BF), "from_x": V((total, features), BF),
            "from_y": V((total, half), BF), "from_z": V((outer - 1, total // outer, half), BF),
            "vec_in": V((steps, 8, features), F32),
            "local_sems": D((2,)), "kept_sems": D((jobs,)),
        })
        for name, shape in (
            ("ag", (18,)), ("core", (jobs, 2)), ("x", (jobs,)), ("y", (jobs,)), ("z", (jobs, outer - 1)),
            ("az", (jobs, outer - 1)), ("ay", (jobs, outer)), ("vec", (steps,)),
        ):
            scratch[name + "_send"] = D(shape)
            scratch[name + "_recv"] = D(shape)
    else:
        ins["w_all"] = (weights[0], outside)
        outs["down_o"] = (S((hidden, features), BF), outside)
        outs["up_o"] = (S((features, hidden), BF), outside)
        outs["qkv_out_o"] = (S((columns + features, features), BF), outside)
    names = list(ins) + list(outs) + list(scratch)
    found = pl.pallas_call(
        functools.partial(fused_kernel, owned, length, capacity, parts, outer, names),
        out_shape=[v[0] for v in outs.values()],
        in_specs=[v[1] for v in ins.values()],
        out_specs=[v[1] for v in outs.values()],
        scratch_shapes=list(scratch.values()),
        compiler_params=pltpu.CompilerParams(
            vmem_limit_bytes=63 << 20,
            has_side_effects=remote,
            collective_id=0 if remote else None,
        ),
    )(*[v[0] for v in ins.values()])
    return dict(zip(outs, found))


def shards(
    images,
    tokens,
    slot_ids,
    counts,
    w_qkv,
    w_out,
    w_up,
    w_down,
    gain_one,
    bias_one,
    gain_two,
    bias_two,
    w_router,
    cotangent,
):
    features = tokens.shape[2]
    hidden = w_up.shape[1]
    parts = lax.axis_size("head")
    me = lax.axis_index("head")
    small = (gain_one, bias_one, gain_two, bias_two, w_router, cotangent)
    outer = images // 2 if images == 8 and parts == 4 else 0
    if outer:
        found = fused(
            parts, outer, tokens, slot_ids, counts, (w_qkv.T, w_out), w_up, w_down, *small
        )
        grads = found["grads_o"]
        part, rows = hidden // parts, w_out.shape[0]
        down, up, out, qkv, result, grad_tokens = finish(
            grads, (part, features, rows, grads.shape[0] - part - features - rows),
            found["result_o"], found["grad_tokens_o"],
        )
        qkv = qkv.T
        vectors = found["vec_o"]
    else:
        w_all = jnp.concatenate(
            [
                lax.all_gather(w_qkv.T, "head", axis=0, tiled=True),
                lax.all_gather(w_out, "head", axis=0, tiled=True),
            ]
        )
        found = fused(parts, outer, tokens, slot_ids, counts, (w_all,), w_up, w_down, *small)
        columns = w_all.shape[0] - features

        def reduced(matrix, axis=0):
            shard = lax.psum_scatter(matrix, "head", scatter_dimension=axis, tiled=True)
            piece = lax.psum_scatter(shard, "img", scatter_dimension=0, tiled=True)
            return lax.all_gather(piece, "img", axis=0, tiled=True).astype(F32)

        both = found["qkv_out_o"]
        down, up = reduced(found["down_o"]), reduced(found["up_o"], 1)
        out, qkv = reduced(both[columns:]), reduced(both[:columns]).T
        vectors = lax.psum(found["vec_o"], ("img", "head"))
        result, grad_tokens = found["result_o"], found["grad_tokens_o"]
    vectors = lax.dynamic_slice_in_dim(
        vectors, me * (features // parts), features // parts, axis=1
    )
    return (
        result,
        grad_tokens,
        qkv,
        out,
        up,
        down,
        vectors[0],
        vectors[1],
        vectors[2],
        vectors[3],
        vectors[4],
    )


def solution(mesh):
    return jax.shard_map(
        functools.partial(shards, mesh.shape["img"]),
        mesh=mesh,
        in_specs=(
            P(("img", "head"), None, None),
            P(("img", "head"), None),
            P(("img", "head")),
            P(None, "head"),
            P("head", None),
            P(),
            P(),
            P(),
            P(),
            P(),
            P(),
            P(),
            P(("img", "head"), None, None),
        ),
        out_specs=(
            P(("img", "head"), None, None),
            P(("img", "head"), None, None),
            P(None, "head"),
            P("head", None),
            P(None, "head"),
            P("head", None),
            P("head"),
            P("head"),
            P("head"),
            P("head"),
            P("head"),
        ),
        check_vma=False,
    )
```

```python
import functools

import jax
import jax.numpy as jnp
from jax import lax
from jax.experimental import pallas as pl
from jax.experimental.pallas import tpu as pltpu
from jax.sharding import PartitionSpec as P

HEAD_DIM = 64
EPS = 1e-06
BF = jnp.bfloat16
F32 = jnp.float32


def nn(a, b):
    return lax.dot_general(a, b, (((1,), (0,)), ((), ())), preferred_element_type=F32)


def nt(a, b):
    return lax.dot_general(a, b, (((1,), (1,)), ((), ())), preferred_element_type=F32)


def tn(a, b):
    return lax.dot_general(a, b, (((0,), (0,)), ((), ())), preferred_element_type=F32)


def standardise(values):
    average = jnp.mean(values, axis=-1, keepdims=True)
    centred = values - average
    variance = jnp.mean(centred * centred, axis=-1, keepdims=True)
    scale = lax.rsqrt(variance + EPS)
    return centred * scale, scale


def norm_pull(grad, unit, scale, gain):
    inner = grad * gain
    first = jnp.mean(inner, axis=-1, keepdims=True)
    second = jnp.mean(inner * unit, axis=-1, keepdims=True)
    return scale * (inner - first - unit * second)


def split_low(values):
    upper = values.astype(BF)
    return upper, (values - upper.astype(F32)).astype(BF)


def slot_table(slots, length):
    capacity = slots.shape[1]
    return (lax.broadcasted_iota(jnp.int32, (length, capacity), 0) == slots).astype(BF)


def row_gate(picked, w_router, count):
    gate = jax.nn.sigmoid(jnp.sum(picked * w_router, axis=-1, keepdims=True))
    valid = (lax.broadcasted_iota(jnp.int32, gate.shape, 0) < count).astype(F32)
    return gate, valid


def lane_low(shape):
    return lax.broadcasted_iota(jnp.int32, shape, 1) < HEAD_DIM


def head_scores(key_tile, query_tile, low, count):
    scores = nt(key_tile, query_tile)
    seen = lax.broadcasted_iota(jnp.int32, scores.shape, 0) < count
    return jnp.where(seen, scores, -1e30)


def swap_halves(tile):
    return pltpu.roll(tile.astype(F32), HEAD_DIM, 1).astype(BF)


def pair_lanes(pair, t):
    return pl.ds(pl.multiple_of((3 * pair + t) * 2 * HEAD_DIM, 128), 2 * HEAD_DIM)


def pair_tiles(proj, rows, pair):
    tiles = [proj[rows, pair_lanes(pair, t)] for t in range(3)]
    low = lane_low(tiles[0].shape)
    zero = jnp.zeros_like(tiles[0])
    swapped = [swap_halves(tile) for tile in tiles]
    scale = HEAD_DIM ** (-0.5)
    query_a = jnp.where(low, tiles[0], zero) * jnp.asarray(scale, BF)
    query_b = jnp.where(low, swapped[1], zero) * jnp.asarray(scale, BF)
    return tiles, swapped, low, zero, ((swapped[0], query_a), (tiles[2], query_b))

MESH_ID = pl.DeviceIdType.MESH
AG_ROWS = 96


def copy_in(source, target, sem):
    copy = pltpu.make_async_copy(source, target, sem)
    copy.start()
    return copy


def aligned(start, size, unit=16):
    return pl.ds(pl.multiple_of(start, unit), size)


class Place:
    def __init__(self, outer):
        self.head = lax.axis_index("head")
        self.img = lax.axis_index("img")
        self.outer = outer
        self.x, self.c = self.head // 2, self.head % 2
        self.z, self.y = self.img // 2, self.img % 2
        self.own = self.head
        self.across = 2 * (1 - self.x) + self.c
        self.core_at = (self.img, 2 * self.x + 1 - self.c)
        self.x_at = (self.img, self.across)
        self.y_at = (2 * self.z + 1 - self.y, self.head)
        self.low, self.high = self.z % 2, self.z // 2
        self.low_at = (2 * (self.z + 1 - 2 * self.low) + self.y, self.head)
        self.high_at = (2 * (self.z + 2 - 4 * self.high) + self.y, self.head)


def remote(source, target, sems, index, device):
    return pltpu.make_async_remote_copy(
        src_ref=source,
        dst_ref=target,
        send_sem=sems[0].at[index],
        recv_sem=sems[1].at[index],
        device_id=device,
        device_id_type=MESH_ID,
    )


def send(source, target, sems, index, device):
    copy = remote(source, target, sems, index, device)
    copy.start()
    return copy


class Gather:
    def __init__(self, place, whole, w_qkv_t, w_out, sems, local_sems):
        self.p, self.whole, self.sems = place, whole, sems
        self.w = (w_qkv_t, w_out)
        self.sizes = (w_qkv_t.shape[0], w_out.shape[0])
        self.columns = 4 * self.sizes[0]
        self.local_sems = local_sems
        self.split = (self.sizes[0] // 2) // AG_ROWS
        self.steps = self.split + 1

    def part(self, shard, kind, first=0, size=None):
        base = shard * self.sizes[kind] + (self.columns if kind else 0) + first
        return self.whole.at[aligned(base, size or self.sizes[kind])]

    def first_row(self, side, t):
        if t == self.split:
            return side * AG_ROWS
        head = t + self.p.c * (self.split - 1 - 2 * t)
        return (2 * head + side) * AG_ROWS

    def piece(self, shard, side, t):
        return self.part(shard, int(t == self.split), self.first_row(side, t), AG_ROWS)

    def source(self, side, t):
        return self.w[int(t == self.split)].at[aligned(self.first_row(side, t), AG_ROWS)]

    def local(self, k):
        return pltpu.make_async_copy(self.w[k], self.part(self.p.own, k), self.local_sems.at[k])

    def core(self, k):
        return remote(self.w[k], self.part(self.p.own, k), self.sems, k, self.p.core_at)

    def over_x(self, t):
        p = self.p
        return remote(self.source(p.y, t), self.piece(p.own, p.y, t), self.sems, 2 + t, p.x_at)

    def over_y(self, t):
        p = self.p
        block = self.piece(p.across, p.y, t)
        return remote(block, block, self.sems, 2 + self.steps + t, p.y_at)

    def passed(self, t):
        p, n = self.p, self.steps
        side = p.y if t < n else 1 - p.y
        block = self.piece(p.across, side, t % n)
        return remote(block, block, self.sems, 2 + 2 * n + t, p.core_at)

    def begin(self):
        for k in range(2):
            self.local(k).start()
            self.core(k).start()
        for t in range(self.steps):
            self.over_x(t).start()

    def own_half(self):
        for k in range(2):
            self.local(k).wait()
            self.core(k).wait_recv()

    def forward_x(self, t):
        self.over_x(t).wait_recv()
        self.over_y(t).start()
        self.passed(t).start()

    def forward_y(self, t):
        self.over_y(t).wait_recv()
        self.passed(self.steps + t).start()

    def other_half(self, steps):
        for t in steps:
            self.passed(t).wait_recv()
            self.passed(self.steps + t).wait_recv()

    def close(self):
        for k in range(2):
            self.core(k).wait_send()
        for t in range(self.steps):
            self.over_x(t).wait_send()
            self.over_y(t).wait_send()
        for t in range(2 * self.steps):
            self.passed(t).wait_send()


def add_into(block, *others):
    rows = 64 if block.shape[0] % 64 == 0 else 16

    @pl.loop(0, block.shape[0] // rows)
    def _(n):
        part = aligned(n * rows, rows)
        total = block[part, :].astype(F32)
        for other in others:
            total += other[part, :].astype(F32)
        block[part, :] = total.astype(BF)


class Reduce:
    def __init__(self, place, jobs, out, buffers, sems, local_sem):
        self.p, self.out = place, out
        self.blocks = [job[0] for job in jobs]
        self.rows = [job[1] for job in jobs]
        self.target = [job[2] for job in jobs]
        self.base = [sum(self.rows[:j]) for j in range(len(jobs))]
        self.from_core, self.from_x, self.from_y, self.from_low, self.from_high = buffers
        self.core_sems, self.x_sems, self.y_sems, self.z_sems, self.a_sems = sems
        self.local_sem = local_sem
        self.jobs = len(jobs)
        self.sent = []
        self.kept, self.core, self.over_x, self.over_y = {}, {}, {}, {}
        self.over_low, self.over_high = {}, {}
        self.all_high, self.all_low, self.all_y = {}, {}, {}
        self.steps = (
            self.to_y, self.to_low, self.to_high, self.back_high, self.back_low, self.back_y, self.finish
        )
        self.half = out.shape[1] // 2
        self.mine = aligned(place.y * self.half, self.half, 128)
        self.theirs = aligned((1 - place.y) * self.half, self.half, 128)

    def span(self, j):
        return slice(self.base[j], self.base[j] + self.rows[j])

    def ready(self, j):
        p = self.p
        shards = [(1 - p.x), p.x]
        self.core[j] = [
            send(
                self.blocks[j](2 * xx + 1 - p.c), self.from_core.at[xx, self.span(j)],
                self.core_sems, (j, n), p.core_at,
            )
            for n, xx in enumerate(shards)
        ]
        self.sent += self.core[j]

    def to_x(self, j):
        p = self.p
        self.core[j][0].wait_recv()
        block = self.blocks[j](p.across)
        add_into(block, self.from_core.at[1 - p.x, self.span(j)])
        self.over_x[j] = send(block, self.from_x.at[self.span(j)], self.x_sems, j, p.x_at)
        self.sent.append(self.over_x[j])

    def to_y(self, j):
        p = self.p
        self.core[j][1].wait_recv()
        self.over_x[j].wait_recv()
        block = self.blocks[j](p.own)
        add_into(block, self.from_core.at[p.x, self.span(j)], self.from_x.at[self.span(j)])
        self.over_y[j] = send(
            block.at[:, self.theirs], self.from_y.at[self.span(j)], self.y_sems, j, p.y_at
        )
        self.sent.append(self.over_y[j])

    def piece(self, j, ref, base, lanes, level):
        p, rows = self.p, self.rows[j]
        if level == 0:
            return ref.at[aligned(base, rows), lanes]
        if level == 1:
            return ref.at[aligned(base + p.low * (rows // 2), rows // 2), lanes]
        return ref.at[aligned(base + p.low * (rows // 2) + p.high * (rows // 4), rows // 4), lanes]

    def to_low(self, j):
        p, half = self.p, self.rows[j] // 2
        self.over_y[j].wait_recv()
        block = self.blocks[j](p.own).at[:, self.mine]
        add_into(block, self.from_y.at[self.span(j)])
        base = self.base[j] // 2
        self.over_low[j] = send(
            block.at[aligned((1 - p.low) * half, half)], self.from_low.at[base : base + half],
            self.z_sems, (j, 0), p.low_at,
        )
        self.sent.append(self.over_low[j])

    def to_high(self, j):
        p, quarter = self.p, self.rows[j] // 4
        self.over_low[j].wait_recv()
        block = self.blocks[j](p.own)
        base = self.base[j] // 2
        add_into(
            self.piece(j, block, 0, self.mine, 1), self.from_low.at[base : base + 2 * quarter]
        )
        base = self.base[j] // 4
        self.over_high[j] = send(
            block.at[aligned(p.low * 2 * quarter + (1 - p.high) * quarter, quarter), self.mine],
            self.from_high.at[base : base + quarter], self.z_sems, (j, 1), p.high_at,
        )
        self.sent.append(self.over_high[j])

    def spread(self, j, level, device, index):
        block = self.piece(j, self.out, self.target[j], self.mine, level)
        source = block
        if level == 2:
            source = self.piece(j, self.blocks[j](self.p.own), 0, self.mine, 2)
        copy = send(source, block, self.a_sems, (j, index), device)
        self.sent.append(copy)
        return copy

    def back_high(self, j):
        self.over_high[j].wait_recv()
        piece = self.piece(j, self.blocks[j](self.p.own), 0, self.mine, 2)
        base, quarter = self.base[j] // 4, self.rows[j] // 4
        add_into(piece, self.from_high.at[base : base + quarter])
        target = self.piece(j, self.out, self.target[j], self.mine, 2)
        self.kept[j] = copy_in(piece, target, self.local_sem.at[j])
        self.all_high[j] = self.spread(j, 2, self.p.high_at, 0)

    def back_low(self, j):
        self.all_high[j].wait_recv()
        self.kept[j].wait()
        self.all_low[j] = self.spread(j, 1, self.p.low_at, 1)

    def back_y(self, j):
        self.all_low[j].wait_recv()
        self.all_y[j] = self.spread(j, 0, self.p.y_at, 2)

    def finish(self, j):
        self.all_y[j].wait_recv()

    def feed(self, last):
        for j in range(min(last + 1, self.jobs)):
            if j in self.core and j not in self.over_x:
                self.to_x(j)

    def tick(self, t):
        for lag, step in enumerate(self.steps):
            if 0 <= t - lag < self.jobs:
                step(t - lag)

    def close(self):
        for copy in self.sent:
            copy.wait_send()


def sum_vectors(place, vec, inbox, sems, sent):
    p = place
    partners = [p.core_at, p.x_at, p.y_at, p.low_at, p.high_at]
    count = len(partners)
    copies = []

    def stage(n):
        if n:
            copies[n - 1].wait_recv()
            vec[n] = vec[n - 1] + inbox[n - 1]
        if n < count:
            copies.append(send(vec.at[n], inbox.at[n], sems, n, partners[n]))
            sent.append(copies[n])

    return [functools.partial(stage, n) for n in range(count + 1)]


def fused_kernel(owned, length, capacity, parts, outer, names, *refs):
    r = dict(zip(names, refs))
    remote = outer > 0
    slots, counts = r["slots"], r["counts"]
    gain_one, bias_one, gain_two, bias_two, w_router = (
        r[k][...][None, :] for k in ("gain_one", "bias_one", "gain_two", "bias_two", "w_router")
    )
    tokens, cotangent = r["tokens"], r["cotangent"]
    wu, wd, ra, rs, down = r["wu"], r["wd"], r["ra"], r["rs"], r["down"]
    normed_two, grad_mlp, mixed, attn, wide = (
        r[k] for k in ("normed_two", "grad_mlp", "mixed", "attn", "wide")
    )
    picked, picked_grad, totals, logits = (r[k] for k in ("picked", "picked_grad", "totals", "logits"))
    tok, cot, res, gtok = (r[k] for k in ("tok", "cot", "res", "gtok"))
    sems, tok_sems, cot_sems, res_sems, gtok_sems = (
        r[k] for k in ("sems", "tok_sems", "cot_sems", "res_sems", "gtok_sems")
    )
    result_o, grad_tokens_o, saved_o, vec_o = (
        r[k] for k in ("result_o", "grad_tokens_o", "saved_o", "vec_o")
    )
    vec = r["vec"]
    features, hidden = wu.shape
    columns = wd.shape[0] - features
    pairs = columns // (6 * HEAD_DIM)
    proj = ra.at[:, 0:columns]
    normed_one = ra.at[:, columns : columns + features]
    width = features // 3
    part = hidden // parts
    rows_all = owned * capacity
    piece = features // 3

    def rows_of(i):
        return aligned(i * capacity, capacity)

    def slot_row(i):
        return slots[pl.ds(i, 1), :]

    def token_copy(i, slot):
        return pltpu.make_async_copy(tokens.at[i], tok.at[slot], tok_sems.at[slot])

    def cot_copy(i, slot):
        return pltpu.make_async_copy(cotangent.at[i], cot.at[slot], cot_sems.at[slot])

    def result_copy(i, slot):
        return pltpu.make_async_copy(res.at[slot], result_o.at[i], res_sems.at[slot])

    def gtok_copy(i, slot):
        return pltpu.make_async_copy(gtok.at[slot], grad_tokens_o.at[i], gtok_sems.at[slot])

    token_copy(0, 0).start()
    cot_copy(0, 0).start()
    reduce = None
    if remote:
        place = Place(outer)
        barrier = pltpu.get_barrier_semaphore()
        partners = [place.core_at, place.x_at, place.y_at, place.low_at, place.high_at]
        for partner in partners:
            pl.semaphore_signal(barrier, inc=1, device_id=partner, device_id_type=MESH_ID)
        pl.semaphore_wait(barrier, len(partners))
        gather = Gather(
            place, down, r["w_qkv_t"], r["w_out"], (r["ag_send"], r["ag_recv"]), r["local_sems"]
        )
        gather.begin()
        w_all = r["w_saved_o"]

        def rows_block(ref, base, step, rows):
            return lambda s: ref.at[aligned(s * step + base, rows)]

        def lanes_block(ref, base, rows):
            return lambda s: ref.at[base : base + rows, aligned(s * part, part, 128)]

        def head_block(ref, q, rows):
            return lambda s: ref.at[aligned(s * share + lax.rem(q + s % 2, 3) * rows, rows)]

        share = columns // parts
        out_rows = features // parts
        jobs = [
            (rows_block(down, piece * k, part, piece), piece, piece * k) for k in range(part // piece)
        ]
        jobs += [
            (lanes_block(wu, piece * k, piece), piece, part + piece * k) for k in range(features // piece)
        ]
        after = part + features
        jobs += [(rows_block(wd, columns, out_rows, out_rows), out_rows, after)]
        after += out_rows
        jobs += [
            (head_block(wd, q, share // 3), share // 3, after + lax.rem(q + place.c, 3) * (share // 3))
            for q in range(3)
        ]
        reduce = Reduce(
            place, jobs, r["grads_o"], [r[k] for k in ("from_core", "from_x", "from_y", "from_low", "from_high")],
            [(r[k + "_send"], r[k + "_recv"]) for k in ("core", "x", "y", "z", "a")],
            r["kept_sems"],
        )
        job_down, job_up = part // piece, features // piece
    else:
        job_down, job_up = part // piece, 3
        w_all = r["w_all"]
        load_w = copy_in(w_all, down, sems.at[0])
    load_up = copy_in(r["w_up"], wu, sems.at[1])
    load_down = copy_in(r["w_down"], wd, sems.at[2])
    ticks = [0]

    def tick():
        if remote:
            reduce.tick(ticks[0])
            ticks[0] += 1

    @pl.loop(0, owned)
    def _(i):
        slot = lax.rem(i, 2)

        @pl.when(i + 1 < owned)
        def _():
            token_copy(i + 1, 1 - slot).start()
            cot_copy(i + 1, 1 - slot).start()

        rows = rows_of(i)
        table = slot_table(slot_row(i), length)
        token_copy(i, slot).wait()
        rows_f = tn(table, tok[slot])
        picked[rows, :] = rows_f.astype(BF)
        unit, _ = standardise(rows_f)
        normed_one[rows, :] = (unit * gain_one + bias_one).astype(BF)
        gate, valid = row_gate(rows_f, w_router, counts[i])
        cot_copy(i, slot).wait()
        grads = tn(table, cot[slot])
        picked_grad[rows, :] = grads.astype(BF)
        grad_mlp[rows, :] = (gate * valid * grads).astype(BF)

    def project(start, size):
        step = rows_all // 3

        @pl.loop(0, 3)
        def _(n):
            rows = aligned(n * step, step)
            cols = pl.ds(pl.multiple_of(start, 128), size)
            proj[rows, cols] = nt(normed_one[rows, :], down[cols, :]).astype(BF)

    def attend(half, chosen, i):
        rows = rows_of(i)
        for p in chosen:
            pair = half * (pairs // 2) + p
            tiles, swapped, low, zero, heads = pair_tiles(proj, rows, pair)
            outs = []
            for h, (key_tile, query_tile) in enumerate(heads):
                scores = head_scores(key_tile, query_tile, low, counts[i])
                highest = jnp.max(scores, axis=0, keepdims=True)
                terms = jnp.exp(scores - highest)
                total = jnp.sum(terms, axis=0, keepdims=True)
                probs = (terms * (1.0 / total)).astype(BF)
                totals[i, pl.ds(2 * pair + h, 1), :] = highest + jnp.log(total)
                outs.append(tn(probs, tiles[1 + h]))
            mixed[rows, aligned(2 * HEAD_DIM * pair, 2 * HEAD_DIM, 128)] = jnp.where(
                low, outs[0], outs[1]
            ).astype(BF)

    half_columns = columns // 2
    pair_columns = 6 * HEAD_DIM
    if remote:
        gather.forward_x(0)
        gather.own_half()
        mine, other = place.x, 1 - place.x
    else:
        load_w.wait()
        mine, other = 0, 1
    project(mine * half_columns, half_columns)

    @pl.loop(0, owned // 2)
    def _(n):
        i = 2 * n
        if remote:
            for at, steps in ((0, ((0, 1),)), (2, ((0, 2), (1, 0))), (4, ((1, 1),))):

                @pl.when(i == at)
                def _(steps=steps):
                    for kind, t in steps:
                        (gather.forward_y if kind else gather.forward_x)(t)

        attend(mine, range(pairs // 2), i)
        attend(mine, range(pairs // 2), i + 1)

    if remote:
        gather.other_half((0, 1))
    for p in (0, 2):
        project(other * half_columns + p * pair_columns, pair_columns)

    if remote:
        gather.forward_x(3)

    @pl.loop(0, owned // 2)
    def _(n):
        if remote:

            @pl.when(n == 1)
            def _():
                gather.forward_y(2)

            @pl.when(n == 2)
            def _():
                gather.forward_y(3)

        attend(other, (0, 2), 2 * n)
        attend(other, (0, 2), 2 * n + 1)

    if remote:
        gather.other_half((2,))
    project(other * half_columns + pair_columns, pair_columns)

    @pl.loop(0, owned // 3)
    def _(n):
        for k in range(3):
            attend(other, (1,), 3 * n + k)

    if remote:
        gather.other_half((gather.split,))
        keep_w = copy_in(down, w_all, sems.at[0])
    save = copy_in(ra, saved_o, sems.at[3])

    @pl.loop(0, 3)
    def _(n):
        cols = aligned(n * width, width, 128)
        attn[:, cols] = nn(mixed[...], down[columns : columns + features, cols])

    @pl.loop(0, owned)
    def _(i):
        rows = rows_of(i)
        unit, _ = standardise(picked[rows, :].astype(F32) + attn[rows, :])
        normed_two[rows, :] = (unit * gain_two + bias_two).astype(BF)

    save.wait()
    load_up.wait()
    step = hidden // 6
    for k in range(part // piece):

        @pl.loop(0, parts)
        def _(h):
            cols = aligned(h * part + k * piece, piece, 128)
            pre = nn(normed_two[...], wu[:, cols])
            below = 0.5 + 0.5 * lax.erf(pre * (0.5**0.5))
            ra[:, cols] = (pre * below).astype(BF)
            rs[:, cols] = (below + pre * (jnp.exp(-0.5 * pre * pre) * 0.3989422804014327)).astype(BF)

        if remote and k == 0:
            gather.close()
            keep_w.wait()
        if remote and k:
            reduce.feed(k - 1)

        @pl.loop(0, parts)
        def _(h):
            cols = aligned(h * part + k * piece, piece, 128)
            down[cols, :] = tn(ra[:, cols], grad_mlp[...]).astype(BF)

        if remote:
            reduce.ready(k)

    if not remote:
        put_down = copy_in(down, r["down_o"], sems.at[4])
    load_down.wait()

    @pl.loop(0, 6)
    def _(n):
        cols = aligned(n * step, step, 128)
        rs[:, cols] = (nt(grad_mlp[...], wd[cols, :]) * rs[:, cols].astype(F32)).astype(BF)

    if remote:
        reduce.feed(job_down - 1)

    @pl.loop(0, 3)
    def _(n):
        cols = aligned(n * width, width, 128)
        wide[:, cols] = nt(rs[...], wu[cols, :])

    tick()
    step_up = features // job_up
    for k in range(job_up):

        @pl.loop(0, parts)
        def _(h):
            cols = aligned(h * part, part, 128)
            rows = slice(k * step_up, (k + 1) * step_up)
            wu[rows, cols] = tn(normed_two[:, rows], rs[:, cols]).astype(BF)

        if remote:
            if k:
                reduce.feed(job_down + k - 1)
            reduce.ready(job_down + k)

    tick()
    if not remote:
        put_up = copy_in(wu, r["up_o"], sems.at[5])

    blocks = [copy_in(w_all.at[columns : columns + features], rs.at[0:features, 0:features], sems.at[6])]
    for n in range(3):
        blocks.append(
            copy_in(
                w_all.at[n * features : (n + 1) * features],
                rs.at[0:features, (n + 1) * features : (n + 2) * features],
                sems.at[7 + n],
            )
        )

    vec[0] = jnp.zeros_like(vec[0])

    @pl.loop(0, owned)
    def _(i):
        rows = rows_of(i)
        rows_f = picked[rows, :].astype(F32)
        unit, scale = standardise(rows_f + attn[rows, :])
        grad = wide[rows, :]
        vec[0, 2:3, :] += jnp.sum(grad * unit, axis=0, keepdims=True)
        vec[0, 3:4, :] += jnp.sum(grad, axis=0, keepdims=True)
        wide[rows, :] = norm_pull(grad, unit, scale, gain_two)

    @pl.loop(0, 3)
    def _(n):
        cols = aligned(n * width, width, 128)
        attn[:, cols] += nn(ra[...], wd[:, cols])

    reload = copy_in(saved_o, ra, sems.at[3])
    if remote:
        reduce.feed(job_down + job_up - 1)
    tick()

    @pl.loop(0, owned)
    def _(i):
        rows = rows_of(i)
        rows_f = picked[rows, :].astype(F32)
        gate, valid = row_gate(rows_f, w_router, counts[i])
        grads = picked_grad[rows, :].astype(F32)
        grad_mlp[rows, :] = (gate * valid * grads + wide[rows, :]).astype(BF)

    @pl.loop(0, 3)
    def _(n):
        cols = aligned(n * width, width, 128)
        wd[columns : columns + features, cols] = tn(mixed[...], grad_mlp[:, cols]).astype(BF)

    if remote:
        reduce.ready(job_down + job_up)
    blocks[0].wait()
    @pl.loop(0, 3)
    def _(n):
        cols = aligned(n * width, width, 128)
        normed_two[:, cols] = nt(grad_mlp[...], rs[cols, 0:features]).astype(BF)

    tick()
    reload.wait()

    def attend_back(chosen, first, last):
        @pl.loop(first, last)
        def _(i):
            rows = rows_of(i)
            for pair in chosen:
                tiles, swapped, low, zero, heads = pair_tiles(proj, rows, pair)
                lanes = slice(2 * HEAD_DIM * pair, 2 * HEAD_DIM * (pair + 1))
                grads = normed_two[rows, lanes]
                halves = (jnp.where(low, grads, zero), jnp.where(low, zero, grads))
                found = []
                for h, (key_tile, query_tile) in enumerate(heads):
                    scores = head_scores(key_tile, query_tile, low, counts[i])
                    probs = jnp.exp(scores - totals[i, 2 * pair + h : 2 * pair + h + 1, :])
                    grad_probs = nt(tiles[1 + h], halves[h])
                    shift = jnp.sum(probs * grad_probs, axis=0, keepdims=True)
                    grad_scores = (probs * (grad_probs - shift)).astype(BF)
                    grad_value = nn(probs.astype(BF), grads)
                    scale = HEAD_DIM ** (-0.5)
                    grad_query = tn(grad_scores, swapped[2 * h]) * scale
                    grad_key = nn(grad_scores, swapped[h]) * scale
                    found.append((grad_query, grad_key, grad_value))
                (query_a, key_a, value_a), (query_b, key_b, value_b) = found
                proj[rows, pair_lanes(pair, 0)] = jnp.where(low, query_a, key_a).astype(BF)
                proj[rows, pair_lanes(pair, 1)] = jnp.where(low, value_a, query_b).astype(BF)
                proj[rows, pair_lanes(pair, 2)] = jnp.where(low, key_b, value_b).astype(BF)

    early = [p for p in range(pairs) if p % 3 != 1]
    late = [p for p in range(pairs) if p % 3 == 1]

    def grad_qkv(count, pair_at):
        @pl.loop(0, count)
        def _(n):
            cols = aligned(pair_at(n) * 6 * HEAD_DIM, 6 * HEAD_DIM, 128)
            wd[cols, :] = tn(proj[:, cols], normed_one[...]).astype(BF)

    if remote:
        reduce.feed(job_down + job_up)
    for n in range(3):
        attend_back(early, n * owned // 3, (n + 1) * owned // 3)
        if n < 2:
            tick()
    grad_qkv(len(early), lambda n: n + (n + 1) // 2)
    first_qkv = job_down + job_up + 1
    if remote:
        reduce.ready(first_qkv)
        reduce.ready(first_qkv + 1)
    tick()
    if remote:
        reduce.feed(first_qkv + 1)
    attend_back(late, 0, owned)
    grad_qkv(len(late), lambda n: 3 * n + 1)
    if remote:
        reduce.ready(first_qkv + 2)
    tick()
    if remote:
        reduce.feed(first_qkv + 2)
    if not remote:
        put_qkv = copy_in(wd, r["qkv_out_o"], sems.at[0])

    for n in range(3):
        blocks[1 + n].wait()
    token_copy(0, 0).start()

    def put_results(first, last):
        @pl.loop(first, last)
        def _(i):
            slot = lax.rem(i, 2)

            @pl.when(i + 1 < owned)
            def _():
                token_copy(i + 1, 1 - slot).start()

            rows = rows_of(i)
            rows_f = picked[rows, :].astype(F32)
            gate, valid = row_gate(rows_f, w_router, counts[i])
            branch = attn[rows, :]
            logit = valid * gate * (1.0 - gate) * jnp.sum(
                picked_grad[rows, :].astype(F32) * branch, axis=-1, keepdims=True
            )
            logits[rows, :] = jnp.broadcast_to(logit, (capacity, 128))
            vec[0, 4:5, :] += jnp.sum(logit * rows_f, axis=0, keepdims=True)
            table = slot_table(slot_row(i), length)
            upper, lower = split_low(gate * valid * branch)
            token_copy(i, slot).wait()

            @pl.when(i >= 2)
            def _():
                result_copy(i - 2, slot).wait()

            res[slot] = (tok[slot].astype(F32) + (nn(table, upper) + nn(table, lower))).astype(BF)
            result_copy(i, slot).start()

    put_results(0, owned // 2)
    tick()
    put_results(owned // 2, owned)

    @pl.loop(0, 3)
    def _(n):
        cols = aligned(n * width, width, 128)
        total = nn(proj[:, 0:features], rs[0:features, aligned(features + n * width, width, 128)])
        for k in range(1, 3):
            total += nn(
                proj[:, k * features : (k + 1) * features],
                rs[0:features, aligned((k + 1) * features + n * width, width, 128)],
            )
        attn[:, cols] = total

    cot_copy(0, 0).start()

    def put_gradients(first, last):
        @pl.loop(first, last)
        def _(i):
            slot = lax.rem(i, 2)

            @pl.when(i + 1 < owned)
            def _():
                cot_copy(i + 1, 1 - slot).start()

            rows = rows_of(i)
            rows_f = picked[rows, :].astype(F32)
            unit, scale = standardise(rows_f)
            grad = attn[rows, :]
            vec[0, 0:1, :] += jnp.sum(grad * unit, axis=0, keepdims=True)
            vec[0, 1:2, :] += jnp.sum(grad, axis=0, keepdims=True)
            back = norm_pull(grad, unit, scale, gain_one)
            total = back + wide[rows, :] + logits[rows, 0:1] * w_router
            table = slot_table(slot_row(i), length)
            upper, lower = split_low(total)
            cot_copy(i, slot).wait()

            @pl.when(i >= 2)
            def _():
                gtok_copy(i - 2, slot).wait()

            gtok[slot] = cot[slot].astype(F32) + (nn(table, upper) + nn(table, lower))
            gtok_copy(i, slot).start()

    put_gradients(0, owned // 2)
    tick()
    put_gradients(owned // 2, owned)

    if remote:
        stages = sum_vectors(place, vec, r["vec_in"], (r["vec_send"], r["vec_recv"]), reduce.sent)
        while ticks[0] < reduce.jobs + len(reduce.steps) - 1:
            if stages:
                stages.pop(0)()
            tick()
        while stages:
            stages.pop(0)()
        vec_o[...] = vec[vec.shape[0] - 1]
    else:
        vec_o[...] = vec[0]

    for i in range(max(owned - 2, 0), owned):
        result_copy(i, i % 2).wait()
        gtok_copy(i, i % 2).wait()
    if remote:
        reduce.close()
    else:
        put_down.wait()
        put_up.wait()
        put_qkv.wait()


def finish_kernel(sizes, *refs):
    grads, result, grad_tokens = refs[:3]
    outs, result_o, grad_tokens_o = refs[3:7], refs[7], refs[8]
    narrow, wide, kept_rows, kept_grads, in_sems, out_sems, row_sems = refs[9:]
    rows_in = [copy_in(result, kept_rows, row_sems.at[0]), copy_in(grad_tokens, kept_grads, row_sems.at[1])]
    chunk = 192
    places = [(out, r) for out, size in zip(outs, sizes) for r in range(0, size, chunk)]
    loads, copies = [], []
    for n in range(len(places)):
        rows = slice(n * chunk, (n + 1) * chunk)
        loads.append(copy_in(grads.at[rows], narrow.at[rows], in_sems.at[n]))
    for n, (out, r) in enumerate(places):
        rows = slice(n * chunk, (n + 1) * chunk)
        loads[n].wait()
        wide[rows, :] = narrow[rows, :].astype(F32)
        copies.append(copy_in(wide.at[rows], out.at[r : r + chunk], out_sems.at[n]))
        if n == 0:
            rows_in[0].wait()
            copies.append(copy_in(kept_rows, result_o, row_sems.at[2]))
            rows_in[1].wait()
            copies.append(copy_in(kept_grads, grad_tokens_o, row_sems.at[3]))
    for copy in copies:
        copy.wait()


def finish(grads, sizes, result, grad_tokens):
    total, features = grads.shape
    outside = pl.BlockSpec(memory_space=pltpu.HBM)
    S = jax.ShapeDtypeStruct
    D = pltpu.SemaphoreType.DMA
    shapes = [S((size, features), F32) for size in sizes]
    shapes += [S(result.shape, result.dtype), S(grad_tokens.shape, grad_tokens.dtype)]
    return pl.pallas_call(
        functools.partial(finish_kernel, sizes),
        out_shape=shapes,
        in_specs=[outside] * 3,
        out_specs=[outside] * len(shapes),
        scratch_shapes=[
            pltpu.VMEM((total, features), BF), pltpu.VMEM((total, features), F32),
            pltpu.VMEM(result.shape, BF), pltpu.VMEM(grad_tokens.shape, F32),
            D((total // 192,)), D((total // 192,)), D((4,)),
        ],
        compiler_params=pltpu.CompilerParams(vmem_limit_bytes=60 << 20),
    )(grads, result, grad_tokens)


def fused(
    parts, outer, tokens, slot_ids, counts, weights, w_up, w_down,
    gain_one, bias_one, gain_two, bias_two, w_router, cotangent,
):
    owned, length, features = tokens.shape
    capacity = slot_ids.shape[1]
    rows = owned * capacity
    hidden = w_up.shape[1]
    remote = outer > 0
    columns = weights[0].shape[0] * parts if remote else weights[0].shape[0] - features
    heads = columns // (3 * HEAD_DIM)
    S = jax.ShapeDtypeStruct
    inside = pl.BlockSpec(memory_space=pltpu.VMEM)
    outside = pl.BlockSpec(memory_space=pltpu.HBM)
    scalars = pl.BlockSpec(memory_space=pltpu.SMEM)
    V = pltpu.VMEM
    D = pltpu.SemaphoreType.DMA
    ins = {
        "slots": (slot_ids, inside), "counts": (counts, scalars),
        "gain_one": (gain_one, inside), "bias_one": (bias_one, inside), "gain_two": (gain_two, inside),
        "bias_two": (bias_two, inside), "w_router": (w_router, inside),
        "tokens": (tokens, outside), "cotangent": (cotangent, outside),
        "w_up": (w_up, outside), "w_down": (w_down, outside),
    }
    outs = {
        "result_o": (S((owned, length, features), BF), outside),
        "grad_tokens_o": (S((owned, length, features), F32), outside),
        "vec_o": (S((8, features), F32), inside),
        "saved_o": (S((rows, columns + features), BF), outside),
    }
    steps = 3
    if remote:
        steps = 5
    scratch = {
        "wu": V((features, hidden), BF), "wd": V((hidden, features), BF), "ra": V((rows, hidden), BF),
        "rs": V((rows, hidden), BF), "down": V((hidden, features), BF),
        "normed_two": V((rows, features), BF), "grad_mlp": V((rows, features), BF),
        "mixed": V((rows, features), BF), "attn": V((rows, features), F32), "wide": V((rows, features), F32),
        "picked": V((rows, features), BF), "picked_grad": V((rows, features), BF),
        "totals": V((owned, heads, capacity), F32), "logits": V((rows, 128), F32),
        "tok": V((2, length, features), BF), "cot": V((2, length, features), BF),
        "res": V((2, length, features), BF), "gtok": V((2, length, features), F32),
        "vec": V((steps + 1, 8, features), F32),
        "sems": D((10,)), "tok_sems": D((2,)), "cot_sems": D((2,)), "res_sems": D((2,)), "gtok_sems": D((2,)),
    }
    if remote:
        ins["w_qkv_t"] = (weights[0], outside)
        ins["w_out"] = (weights[1], outside)
        outs["w_saved_o"] = (S((columns + features, features), BF), outside)
        total = (columns + features + 2 * hidden) // parts
        jobs = 10
        outs["grads_o"] = (S((total, features), BF), outside)
        half = features // 2
        scratch.update({
            "from_core": V((2, total, features), BF), "from_x": V((total, features), BF),
            "from_y": V((total, half), BF), "from_low": V((total // 2, half), BF),
            "from_high": V((total // 4, half), BF),
            "vec_in": V((steps, 8, features), F32),
            "local_sems": D((2,)), "kept_sems": D((jobs,)),
        })
        for name, shape in (
            ("ag", (18,)), ("core", (jobs, 2)), ("x", (jobs,)), ("y", (jobs,)), ("z", (jobs, 2)),
            ("a", (jobs, 3)), ("vec", (steps,)),
        ):
            scratch[name + "_send"] = D(shape)
            scratch[name + "_recv"] = D(shape)
    else:
        ins["w_all"] = (weights[0], outside)
        outs["down_o"] = (S((hidden, features), BF), outside)
        outs["up_o"] = (S((features, hidden), BF), outside)
        outs["qkv_out_o"] = (S((columns + features, features), BF), outside)
    names = list(ins) + list(outs) + list(scratch)
    found = pl.pallas_call(
        functools.partial(fused_kernel, owned, length, capacity, parts, outer, names),
        out_shape=[v[0] for v in outs.values()],
        in_specs=[v[1] for v in ins.values()],
        out_specs=[v[1] for v in outs.values()],
        scratch_shapes=list(scratch.values()),
        compiler_params=pltpu.CompilerParams(
            vmem_limit_bytes=63 << 20,
            has_side_effects=remote,
            collective_id=0 if remote else None,
        ),
    )(*[v[0] for v in ins.values()])
    return dict(zip(outs, found))


def shards(
    images,
    tokens,
    slot_ids,
    counts,
    w_qkv,
    w_out,
    w_up,
    w_down,
    gain_one,
    bias_one,
    gain_two,
    bias_two,
    w_router,
    cotangent,
):
    features = tokens.shape[2]
    hidden = w_up.shape[1]
    parts = lax.axis_size("head")
    me = lax.axis_index("head")
    small = (gain_one, bias_one, gain_two, bias_two, w_router, cotangent)
    outer = images // 2 if images == 8 and parts == 4 else 0
    if outer:
        found = fused(
            parts, outer, tokens, slot_ids, counts, (w_qkv.T, w_out), w_up, w_down, *small
        )
        grads = found["grads_o"]
        part, rows = hidden // parts, w_out.shape[0]
        down, up, out, qkv, result, grad_tokens = finish(
            grads, (part, features, rows, grads.shape[0] - part - features - rows),
            found["result_o"], found["grad_tokens_o"],
        )
        qkv = qkv.T
        vectors = found["vec_o"]
    else:
        w_all = jnp.concatenate(
            [
                lax.all_gather(w_qkv.T, "head", axis=0, tiled=True),
                lax.all_gather(w_out, "head", axis=0, tiled=True),
            ]
        )
        found = fused(parts, outer, tokens, slot_ids, counts, (w_all,), w_up, w_down, *small)
        columns = w_all.shape[0] - features

        def reduced(matrix, axis=0):
            shard = lax.psum_scatter(matrix, "head", scatter_dimension=axis, tiled=True)
            piece = lax.psum_scatter(shard, "img", scatter_dimension=0, tiled=True)
            return lax.all_gather(piece, "img", axis=0, tiled=True).astype(F32)

        both = found["qkv_out_o"]
        down, up = reduced(found["down_o"]), reduced(found["up_o"], 1)
        out, qkv = reduced(both[columns:]), reduced(both[:columns]).T
        vectors = lax.psum(found["vec_o"], ("img", "head"))
        result, grad_tokens = found["result_o"], found["grad_tokens_o"]
    vectors = lax.dynamic_slice_in_dim(
        vectors, me * (features // parts), features // parts, axis=1
    )
    return (
        result,
        grad_tokens,
        qkv,
        out,
        up,
        down,
        vectors[0],
        vectors[1],
        vectors[2],
        vectors[3],
        vectors[4],
    )


def solution(mesh):
    return jax.shard_map(
        functools.partial(shards, mesh.shape["img"]),
        mesh=mesh,
        in_specs=(
            P(("img", "head"), None, None),
            P(("img", "head"), None),
            P(("img", "head")),
            P(None, "head"),
            P("head", None),
            P(),
            P(),
            P(),
            P(),
            P(),
            P(),
            P(),
            P(("img", "head"), None, None),
        ),
        out_specs=(
            P(("img", "head"), None, None),
            P(("img", "head"), None, None),
            P(None, "head"),
            P("head", None),
            P(None, "head"),
            P("head", None),
            P("head"),
            P("head"),
            P("head"),
            P("head"),
            P("head"),
        ),
        check_vma=False,
    )
```

```python
import functools

import jax
import jax.numpy as jnp
from jax import lax
from jax.experimental import pallas as pl
from jax.experimental.pallas import tpu as pltpu
from jax.sharding import PartitionSpec as P

HEAD_DIM = 64
EPS = 1e-06
BF = jnp.bfloat16
F32 = jnp.float32


def nn(a, b):
    return lax.dot_general(a, b, (((1,), (0,)), ((), ())), preferred_element_type=F32)


def nt(a, b):
    return lax.dot_general(a, b, (((1,), (1,)), ((), ())), preferred_element_type=F32)


def tn(a, b):
    return lax.dot_general(a, b, (((0,), (0,)), ((), ())), preferred_element_type=F32)


def standardise(values):
    average = jnp.mean(values, axis=-1, keepdims=True)
    centred = values - average
    variance = jnp.mean(centred * centred, axis=-1, keepdims=True)
    scale = lax.rsqrt(variance + EPS)
    return centred * scale, scale


def norm_pull(grad, unit, scale, gain):
    inner = grad * gain
    first = jnp.mean(inner, axis=-1, keepdims=True)
    second = jnp.mean(inner * unit, axis=-1, keepdims=True)
    return scale * (inner - first - unit * second)


def split_low(values):
    upper = values.astype(BF)
    return upper, (values - upper.astype(F32)).astype(BF)


def slot_table(slots, length):
    capacity = slots.shape[1]
    return (lax.broadcasted_iota(jnp.int32, (length, capacity), 0) == slots).astype(BF)


def row_gate(picked, w_router, count):
    gate = jax.nn.sigmoid(jnp.sum(picked * w_router, axis=-1, keepdims=True))
    valid = (lax.broadcasted_iota(jnp.int32, gate.shape, 0) < count).astype(F32)
    return gate, valid


def lane_low(shape):
    return lax.broadcasted_iota(jnp.int32, shape, 1) < HEAD_DIM


def head_scores(key_tile, query_tile, low, count):
    scores = nt(key_tile, query_tile)
    seen = lax.broadcasted_iota(jnp.int32, scores.shape, 0) < count
    return jnp.where(seen, scores, -1e30)


def swap_halves(tile):
    return pltpu.roll(tile.astype(F32), HEAD_DIM, 1).astype(BF)


def pair_lanes(pair, t):
    return pl.ds(pl.multiple_of((3 * pair + t) * 2 * HEAD_DIM, 128), 2 * HEAD_DIM)


def pair_tiles(proj, rows, pair):
    tiles = [proj[rows, pair_lanes(pair, t)] for t in range(3)]
    low = lane_low(tiles[0].shape)
    zero = jnp.zeros_like(tiles[0])
    swapped = [swap_halves(tile) for tile in tiles]
    scale = HEAD_DIM ** (-0.5)
    query_a = jnp.where(low, tiles[0], zero) * jnp.asarray(scale, BF)
    query_b = jnp.where(low, swapped[1], zero) * jnp.asarray(scale, BF)
    return tiles, swapped, low, zero, ((swapped[0], query_a), (tiles[2], query_b))

MESH_ID = pl.DeviceIdType.MESH
AG_ROWS = 96


def copy_in(source, target, sem):
    copy = pltpu.make_async_copy(source, target, sem)
    copy.start()
    return copy


def aligned(start, size, unit=16):
    return pl.ds(pl.multiple_of(start, unit), size)


class Place:
    def __init__(self, outer):
        self.head = lax.axis_index("head")
        self.img = lax.axis_index("img")
        self.outer = outer
        self.x, self.c = self.head // 2, self.head % 2
        self.z, self.y = self.img // 2, self.img % 2
        self.own = self.head
        self.across = 2 * (1 - self.x) + self.c
        self.core_at = (self.img, 2 * self.x + 1 - self.c)
        self.x_at = (self.img, self.across)
        self.y_at = (2 * self.z + 1 - self.y, self.head)
        self.low, self.high = self.z % 2, self.z // 2
        self.low_at = (2 * (self.z + 1 - 2 * self.low) + self.y, self.head)
        self.high_at = (2 * (self.z + 2 - 4 * self.high) + self.y, self.head)


def remote(source, target, sems, index, device):
    return pltpu.make_async_remote_copy(
        src_ref=source,
        dst_ref=target,
        send_sem=sems[0].at[index],
        recv_sem=sems[1].at[index],
        device_id=device,
        device_id_type=MESH_ID,
    )


def send(source, target, sems, index, device):
    copy = remote(source, target, sems, index, device)
    copy.start()
    return copy


class Gather:
    def __init__(self, place, whole, w_qkv_t, w_out, sems, local_sems):
        self.p, self.whole, self.sems = place, whole, sems
        self.w = (w_qkv_t, w_out)
        self.sizes = (w_qkv_t.shape[0], w_out.shape[0])
        self.columns = 4 * self.sizes[0]
        self.local_sems = local_sems
        self.split = (self.sizes[0] // 2) // AG_ROWS
        self.steps = self.split + 1

    def part(self, shard, kind, first=0, size=None):
        base = shard * self.sizes[kind] + (self.columns if kind else 0) + first
        return self.whole.at[aligned(base, size or self.sizes[kind])]

    def first_row(self, side, t):
        if t == self.split:
            return side * AG_ROWS
        head = t + self.p.c * (self.split - 1 - 2 * t)
        return (2 * head + side) * AG_ROWS

    def piece(self, shard, side, t):
        return self.part(shard, int(t == self.split), self.first_row(side, t), AG_ROWS)

    def source(self, side, t):
        return self.w[int(t == self.split)].at[aligned(self.first_row(side, t), AG_ROWS)]

    def local(self, k):
        return pltpu.make_async_copy(self.w[k], self.part(self.p.own, k), self.local_sems.at[k])

    def core(self, k):
        return remote(self.w[k], self.part(self.p.own, k), self.sems, k, self.p.core_at)

    def over_x(self, t):
        p = self.p
        return remote(self.source(p.y, t), self.piece(p.own, p.y, t), self.sems, 2 + t, p.x_at)

    def over_y(self, t):
        p = self.p
        block = self.piece(p.across, p.y, t)
        return remote(block, block, self.sems, 2 + self.steps + t, p.y_at)

    def passed(self, t):
        p, n = self.p, self.steps
        side = p.y if t < n else 1 - p.y
        block = self.piece(p.across, side, t % n)
        return remote(block, block, self.sems, 2 + 2 * n + t, p.core_at)

    def begin(self):
        for k in range(2):
            self.local(k).start()
            self.core(k).start()
        for t in range(self.steps):
            self.over_x(t).start()

    def own_half(self):
        for k in range(2):
            self.local(k).wait()
            self.core(k).wait_recv()

    def forward_x(self, t):
        self.over_x(t).wait_recv()
        self.over_y(t).start()
        self.passed(t).start()

    def forward_y(self, t):
        self.over_y(t).wait_recv()
        self.passed(self.steps + t).start()

    def other_half(self, steps):
        for t in steps:
            self.passed(t).wait_recv()
            self.passed(self.steps + t).wait_recv()

    def close(self):
        for k in range(2):
            self.core(k).wait_send()
        for t in range(self.steps):
            self.over_x(t).wait_send()
            self.over_y(t).wait_send()
        for t in range(2 * self.steps):
            self.passed(t).wait_send()


def add_into(block, *others):
    rows = 64 if block.shape[0] % 64 == 0 else 16

    @pl.loop(0, block.shape[0] // rows)
    def _(n):
        part = aligned(n * rows, rows)
        total = block[part, :].astype(F32)
        for other in others:
            total += other[part, :].astype(F32)
        block[part, :] = total.astype(BF)


class Reduce:
    def __init__(self, place, jobs, out, buffers, sems, local_sem):
        self.p, self.out = place, out
        self.blocks = [job[0] for job in jobs]
        self.rows = [job[1] for job in jobs]
        self.target = [job[2] for job in jobs]
        self.base = [sum(self.rows[:j]) for j in range(len(jobs))]
        self.from_core, self.from_x, self.from_y, self.from_low, self.from_high = buffers
        self.core_sems, self.x_sems, self.y_sems, self.z_sems, self.a_sems = sems
        self.local_sem = local_sem
        self.jobs = len(jobs)
        self.sent = []
        self.kept, self.core, self.over_x, self.over_y = {}, {}, {}, {}
        self.over_low, self.over_high = {}, {}
        self.all_high, self.all_low, self.all_y = {}, {}, {}
        self.steps = (
            self.to_y, self.to_low, self.to_high, self.back_high, self.back_low, self.back_y, self.finish
        )
        self.half = out.shape[1] // 2
        self.mine = aligned(place.y * self.half, self.half, 128)
        self.theirs = aligned((1 - place.y) * self.half, self.half, 128)

    def span(self, j):
        return slice(self.base[j], self.base[j] + self.rows[j])

    def ready(self, j):
        p = self.p
        shards = [(1 - p.x), p.x]
        self.core[j] = [
            send(
                self.blocks[j](2 * xx + 1 - p.c), self.from_core.at[xx, self.span(j)],
                self.core_sems, (j, n), p.core_at,
            )
            for n, xx in enumerate(shards)
        ]
        self.sent += self.core[j]

    def to_x(self, j):
        p = self.p
        self.core[j][0].wait_recv()
        block = self.blocks[j](p.across)
        add_into(block, self.from_core.at[1 - p.x, self.span(j)])
        self.over_x[j] = send(block, self.from_x.at[self.span(j)], self.x_sems, j, p.x_at)
        self.sent.append(self.over_x[j])

    def to_y(self, j):
        p = self.p
        self.core[j][1].wait_recv()
        self.over_x[j].wait_recv()
        block = self.blocks[j](p.own)
        add_into(block, self.from_core.at[p.x, self.span(j)], self.from_x.at[self.span(j)])
        self.over_y[j] = send(
            block.at[:, self.theirs], self.from_y.at[self.span(j)], self.y_sems, j, p.y_at
        )
        self.sent.append(self.over_y[j])

    def piece(self, j, ref, base, lanes, level):
        p, rows = self.p, self.rows[j]
        if level == 0:
            return ref.at[aligned(base, rows), lanes]
        if level == 1:
            return ref.at[aligned(base + p.low * (rows // 2), rows // 2), lanes]
        return ref.at[aligned(base + p.low * (rows // 2) + p.high * (rows // 4), rows // 4), lanes]

    def to_low(self, j):
        p, half = self.p, self.rows[j] // 2
        self.over_y[j].wait_recv()
        block = self.blocks[j](p.own).at[:, self.mine]
        add_into(block, self.from_y.at[self.span(j)])
        base = self.base[j] // 2
        self.over_low[j] = send(
            block.at[aligned((1 - p.low) * half, half)], self.from_low.at[base : base + half],
            self.z_sems, (j, 0), p.low_at,
        )
        self.sent.append(self.over_low[j])

    def to_high(self, j):
        p, quarter = self.p, self.rows[j] // 4
        self.over_low[j].wait_recv()
        block = self.blocks[j](p.own)
        base = self.base[j] // 2
        add_into(
            self.piece(j, block, 0, self.mine, 1), self.from_low.at[base : base + 2 * quarter]
        )
        base = self.base[j] // 4
        self.over_high[j] = send(
            block.at[aligned(p.low * 2 * quarter + (1 - p.high) * quarter, quarter), self.mine],
            self.from_high.at[base : base + quarter], self.z_sems, (j, 1), p.high_at,
        )
        self.sent.append(self.over_high[j])

    def spread(self, j, level, device, index):
        block = self.piece(j, self.out, self.target[j], self.mine, level)
        source = block
        if level == 2:
            source = self.piece(j, self.blocks[j](self.p.own), 0, self.mine, 2)
        copy = send(source, block, self.a_sems, (j, index), device)
        self.sent.append(copy)
        return copy

    def back_high(self, j):
        self.over_high[j].wait_recv()
        piece = self.piece(j, self.blocks[j](self.p.own), 0, self.mine, 2)
        base, quarter = self.base[j] // 4, self.rows[j] // 4
        add_into(piece, self.from_high.at[base : base + quarter])
        target = self.piece(j, self.out, self.target[j], self.mine, 2)
        self.kept[j] = copy_in(piece, target, self.local_sem.at[j])
        self.all_high[j] = self.spread(j, 2, self.p.high_at, 0)

    def back_low(self, j):
        self.all_high[j].wait_recv()
        self.kept[j].wait()
        self.all_low[j] = self.spread(j, 1, self.p.low_at, 1)

    def back_y(self, j):
        self.all_low[j].wait_recv()
        self.all_y[j] = self.spread(j, 0, self.p.y_at, 2)

    def finish(self, j):
        self.all_y[j].wait_recv()

    def feed(self, last):
        for j in range(min(last + 1, self.jobs)):
            if j in self.core and j not in self.over_x:
                self.to_x(j)

    def tick(self, t):
        for lag, step in enumerate(self.steps):
            if 0 <= t - lag < self.jobs:
                step(t - lag)

    def close(self):
        for copy in self.sent:
            copy.wait_send()


def sum_vectors(place, vec, inbox, sems, sent):
    p = place
    partners = [p.core_at, p.x_at, p.y_at, p.low_at, p.high_at]
    count = len(partners)
    copies = []

    def stage(n):
        if n:
            copies[n - 1].wait_recv()
            vec[n] = vec[n - 1] + inbox[n - 1]
        if n < count:
            copies.append(send(vec.at[n], inbox.at[n], sems, n, partners[n]))
            sent.append(copies[n])

    return [functools.partial(stage, n) for n in range(count + 1)]


def fused_kernel(owned, length, capacity, parts, outer, names, *refs):
    r = dict(zip(names, refs))
    remote = outer > 0
    slots, counts = r["slots"], r["counts"]
    gain_one, bias_one, gain_two, bias_two, w_router = (
        r[k][...][None, :] for k in ("gain_one", "bias_one", "gain_two", "bias_two", "w_router")
    )
    tokens, cotangent = r["tokens"], r["cotangent"]
    wu, wd, ra, rs, down = r["wu"], r["wd"], r["ra"], r["rs"], r["down"]
    normed_two, grad_mlp, mixed, attn, wide = (
        r[k] for k in ("normed_two", "grad_mlp", "mixed", "attn", "wide")
    )
    picked, picked_grad, totals, logits = (r[k] for k in ("picked", "picked_grad", "totals", "logits"))
    tok, cot, res, gtok = (r[k] for k in ("tok", "cot", "res", "gtok"))
    sems, tok_sems, cot_sems, res_sems, gtok_sems = (
        r[k] for k in ("sems", "tok_sems", "cot_sems", "res_sems", "gtok_sems")
    )
    result_o, grad_tokens_o, saved_o, vec_o = (
        r[k] for k in ("result_o", "grad_tokens_o", "saved_o", "vec_o")
    )
    vec = r["vec"]
    features, hidden = wu.shape
    columns = wd.shape[0] - features
    pairs = columns // (6 * HEAD_DIM)
    proj = ra.at[:, 0:columns]
    normed_one = ra.at[:, columns : columns + features]
    width = features // 3
    part = hidden // parts
    rows_all = owned * capacity
    piece = features // 3

    def rows_of(i):
        return aligned(i * capacity, capacity)

    def slot_row(i):
        return slots[pl.ds(i, 1), :]

    def token_copy(i, slot):
        return pltpu.make_async_copy(tokens.at[i], tok.at[slot], tok_sems.at[slot])

    def cot_copy(i, slot):
        return pltpu.make_async_copy(cotangent.at[i], cot.at[slot], cot_sems.at[slot])

    def result_copy(i, slot):
        return pltpu.make_async_copy(res.at[slot], result_o.at[i], res_sems.at[slot])

    def gtok_copy(i, slot):
        return pltpu.make_async_copy(gtok.at[slot], grad_tokens_o.at[i], gtok_sems.at[slot])

    token_copy(0, 0).start()
    cot_copy(0, 0).start()
    reduce = None
    if remote:
        place = Place(outer)
        barrier = pltpu.get_barrier_semaphore()
        partners = [place.core_at, place.x_at, place.y_at, place.low_at, place.high_at]
        for partner in partners:
            pl.semaphore_signal(barrier, inc=1, device_id=partner, device_id_type=MESH_ID)
        pl.semaphore_wait(barrier, len(partners))
        gather = Gather(
            place, down, r["w_qkv_t"], r["w_out"], (r["ag_send"], r["ag_recv"]), r["local_sems"]
        )
        gather.begin()
        w_all = r["w_saved_o"]

        def rows_block(ref, base, step, rows):
            return lambda s: ref.at[aligned(s * step + base, rows)]

        def lanes_block(ref, base, rows):
            return lambda s: ref.at[base : base + rows, aligned(s * part, part, 128)]

        def head_block(ref, q, rows):
            return lambda s: ref.at[aligned(s * share + lax.rem(q + s % 2, 3) * rows, rows)]

        share = columns // parts
        out_rows = features // parts
        jobs = [
            (rows_block(down, piece * k, part, piece), piece, piece * k) for k in range(part // piece)
        ]
        jobs += [
            (lanes_block(wu, piece * k, piece), piece, part + piece * k) for k in range(features // piece)
        ]
        after = part + features
        jobs += [(rows_block(wd, columns, out_rows, out_rows), out_rows, after)]
        after += out_rows
        jobs += [
            (head_block(wd, q, share // 3), share // 3, after + lax.rem(q + place.c, 3) * (share // 3))
            for q in range(3)
        ]
        reduce = Reduce(
            place, jobs, r["grads_o"], [r[k] for k in ("from_core", "from_x", "from_y", "from_low", "from_high")],
            [(r[k + "_send"], r[k + "_recv"]) for k in ("core", "x", "y", "z", "a")],
            r["kept_sems"],
        )
        job_down, job_up = part // piece, features // piece
    else:
        job_down, job_up = part // piece, 3
        w_all = r["w_all"]
        load_w = copy_in(w_all, down, sems.at[0])
    load_up = copy_in(r["w_up"], wu, sems.at[1])
    load_down = copy_in(r["w_down"], wd, sems.at[2])
    ticks = [0]

    def tick():
        if remote:
            reduce.tick(ticks[0])
            ticks[0] += 1

    @pl.loop(0, owned)
    def _(i):
        slot = lax.rem(i, 2)

        @pl.when(i + 1 < owned)
        def _():
            token_copy(i + 1, 1 - slot).start()
            cot_copy(i + 1, 1 - slot).start()

        rows = rows_of(i)
        table = slot_table(slot_row(i), length)
        token_copy(i, slot).wait()
        rows_f = tn(table, tok[slot])
        picked[rows, :] = rows_f.astype(BF)
        unit, _ = standardise(rows_f)
        normed_one[rows, :] = (unit * gain_one + bias_one).astype(BF)
        gate, valid = row_gate(rows_f, w_router, counts[i])
        cot_copy(i, slot).wait()
        grads = tn(table, cot[slot])
        picked_grad[rows, :] = grads.astype(BF)
        grad_mlp[rows, :] = (gate * valid * grads).astype(BF)

    def project(start, size):
        step = rows_all // 3

        @pl.loop(0, 3)
        def _(n):
            rows = aligned(n * step, step)
            cols = pl.ds(pl.multiple_of(start, 128), size)
            proj[rows, cols] = nt(normed_one[rows, :], down[cols, :]).astype(BF)

    def attend(half, chosen, i):
        rows = rows_of(i)
        for p in chosen:
            pair = half * (pairs // 2) + p
            tiles, swapped, low, zero, heads = pair_tiles(proj, rows, pair)
            outs = []
            for h, (key_tile, query_tile) in enumerate(heads):
                scores = head_scores(key_tile, query_tile, low, counts[i])
                highest = jnp.max(scores, axis=0, keepdims=True)
                terms = jnp.exp(scores - highest)
                total = jnp.sum(terms, axis=0, keepdims=True)
                probs = (terms * (1.0 / total)).astype(BF)
                totals[i, pl.ds(2 * pair + h, 1), :] = highest + jnp.log(total)
                outs.append(tn(probs, tiles[1 + h]))
            mixed[rows, aligned(2 * HEAD_DIM * pair, 2 * HEAD_DIM, 128)] = jnp.where(
                low, outs[0], outs[1]
            ).astype(BF)

    half_columns = columns // 2
    pair_columns = 6 * HEAD_DIM
    if remote:
        gather.forward_x(0)
        gather.own_half()
        mine, other = place.x, 1 - place.x
    else:
        load_w.wait()
        mine, other = 0, 1
    project(mine * half_columns, half_columns)

    @pl.loop(0, owned // 2)
    def _(n):
        i = 2 * n
        if remote:
            for at, steps in ((0, ((0, 1),)), (2, ((0, 2), (1, 0))), (4, ((1, 1),))):

                @pl.when(i == at)
                def _(steps=steps):
                    for kind, t in steps:
                        (gather.forward_y if kind else gather.forward_x)(t)

        attend(mine, range(pairs // 2), i)
        attend(mine, range(pairs // 2), i + 1)

    if remote:
        gather.other_half((0, 1))
    for p in (0, 2):
        project(other * half_columns + p * pair_columns, pair_columns)

    if remote:
        gather.forward_x(3)

    @pl.loop(0, owned // 2)
    def _(n):
        if remote:

            @pl.when(n == 1)
            def _():
                gather.forward_y(2)

            @pl.when(n == 2)
            def _():
                gather.forward_y(3)

        attend(other, (0, 2), 2 * n)
        attend(other, (0, 2), 2 * n + 1)

    if remote:
        gather.other_half((2,))
    project(other * half_columns + pair_columns, pair_columns)

    @pl.loop(0, owned // 3)
    def _(n):
        for k in range(3):
            attend(other, (1,), 3 * n + k)

    if remote:
        gather.other_half((gather.split,))
        keep_w = copy_in(down, w_all, sems.at[0])
    save = copy_in(ra, saved_o, sems.at[3])

    @pl.loop(0, 3)
    def _(n):
        cols = aligned(n * width, width, 128)
        attn[:, cols] = nn(mixed[...], down[columns : columns + features, cols])

    @pl.loop(0, owned)
    def _(i):
        rows = rows_of(i)
        unit, _ = standardise(picked[rows, :].astype(F32) + attn[rows, :])
        normed_two[rows, :] = (unit * gain_two + bias_two).astype(BF)

    save.wait()
    load_up.wait()
    step = hidden // 6
    for k in range(part // piece):

        @pl.loop(0, parts)
        def _(h):
            cols = aligned(h * part + k * piece, piece, 128)
            pre = nn(normed_two[...], wu[:, cols])
            below = 0.5 + 0.5 * lax.erf(pre * (0.5**0.5))
            ra[:, cols] = (pre * below).astype(BF)
            rs[:, cols] = (below + pre * (jnp.exp(-0.5 * pre * pre) * 0.3989422804014327)).astype(BF)

        if remote and k == 0:
            gather.close()
            keep_w.wait()
        if remote and k:
            reduce.feed(k - 1)

        @pl.loop(0, parts)
        def _(h):
            cols = aligned(h * part + k * piece, piece, 128)
            down[cols, :] = tn(ra[:, cols], grad_mlp[...]).astype(BF)

        if remote:
            reduce.ready(k)

    if not remote:
        put_down = copy_in(down, r["down_o"], sems.at[4])
    load_down.wait()

    @pl.loop(0, 6)
    def _(n):
        cols = aligned(n * step, step, 128)
        rs[:, cols] = (nt(grad_mlp[...], wd[cols, :]) * rs[:, cols].astype(F32)).astype(BF)

    if remote:
        reduce.feed(job_down - 1)

    @pl.loop(0, 3)
    def _(n):
        cols = aligned(n * width, width, 128)
        wide[:, cols] = nt(rs[...], wu[cols, :])

    tick()
    step_up = features // job_up
    for k in range(job_up):

        @pl.loop(0, parts)
        def _(h):
            cols = aligned(h * part, part, 128)
            rows = slice(k * step_up, (k + 1) * step_up)
            wu[rows, cols] = tn(normed_two[:, rows], rs[:, cols]).astype(BF)

        if remote:
            if k:
                reduce.feed(job_down + k - 1)
            reduce.ready(job_down + k)

    tick()
    if not remote:
        put_up = copy_in(wu, r["up_o"], sems.at[5])

    blocks = [copy_in(w_all.at[columns : columns + features], rs.at[0:features, 0:features], sems.at[6])]
    for n in range(3):
        blocks.append(
            copy_in(
                w_all.at[n * features : (n + 1) * features],
                rs.at[0:features, (n + 1) * features : (n + 2) * features],
                sems.at[7 + n],
            )
        )

    vec[0] = jnp.zeros_like(vec[0])

    @pl.loop(0, owned)
    def _(i):
        rows = rows_of(i)
        rows_f = picked[rows, :].astype(F32)
        unit, scale = standardise(rows_f + attn[rows, :])
        grad = wide[rows, :]
        vec[0, 2:3, :] += jnp.sum(grad * unit, axis=0, keepdims=True)
        vec[0, 3:4, :] += jnp.sum(grad, axis=0, keepdims=True)
        wide[rows, :] = norm_pull(grad, unit, scale, gain_two)

    @pl.loop(0, 3)
    def _(n):
        cols = aligned(n * width, width, 128)
        attn[:, cols] += nn(ra[...], wd[:, cols])

    reload = copy_in(saved_o, ra, sems.at[3])
    if remote:
        reduce.feed(job_down + job_up - 1)
    tick()

    @pl.loop(0, owned)
    def _(i):
        rows = rows_of(i)
        rows_f = picked[rows, :].astype(F32)
        gate, valid = row_gate(rows_f, w_router, counts[i])
        grads = picked_grad[rows, :].astype(F32)
        grad_mlp[rows, :] = (gate * valid * grads + wide[rows, :]).astype(BF)

    @pl.loop(0, 3)
    def _(n):
        cols = aligned(n * width, width, 128)
        wd[columns : columns + features, cols] = tn(mixed[...], grad_mlp[:, cols]).astype(BF)

    if remote:
        reduce.ready(job_down + job_up)
    blocks[0].wait()
    @pl.loop(0, 3)
    def _(n):
        cols = aligned(n * width, width, 128)
        normed_two[:, cols] = nt(grad_mlp[...], rs[cols, 0:features]).astype(BF)

    tick()
    reload.wait()

    def attend_back(chosen, first, last):
        each = 4 // len(chosen) if len(chosen) < 4 else 1

        @pl.loop(first // each, last // each)
        def _(n):
            for i, pair in [(each * n + k, pair) for k in range(each) for pair in chosen]:
                rows = rows_of(i)
                tiles, swapped, low, zero, heads = pair_tiles(proj, rows, pair)
                lanes = slice(2 * HEAD_DIM * pair, 2 * HEAD_DIM * (pair + 1))
                grads = normed_two[rows, lanes]
                halves = (jnp.where(low, grads, zero), jnp.where(low, zero, grads))
                found = []
                for h, (key_tile, query_tile) in enumerate(heads):
                    scores = head_scores(key_tile, query_tile, low, counts[i])
                    probs = jnp.exp(scores - totals[i, 2 * pair + h : 2 * pair + h + 1, :])
                    grad_probs = nt(tiles[1 + h], halves[h])
                    shift = jnp.sum(probs * grad_probs, axis=0, keepdims=True)
                    grad_scores = (probs * (grad_probs - shift)).astype(BF)
                    grad_value = nn(probs.astype(BF), grads)
                    scale = HEAD_DIM ** (-0.5)
                    grad_query = tn(grad_scores, swapped[2 * h]) * scale
                    grad_key = nn(grad_scores, swapped[h]) * scale
                    found.append((grad_query, grad_key, grad_value))
                (query_a, key_a, value_a), (query_b, key_b, value_b) = found
                proj[rows, pair_lanes(pair, 0)] = jnp.where(low, query_a, key_a).astype(BF)
                proj[rows, pair_lanes(pair, 1)] = jnp.where(low, value_a, query_b).astype(BF)
                proj[rows, pair_lanes(pair, 2)] = jnp.where(low, key_b, value_b).astype(BF)

    early = [p for p in range(pairs) if p % 3 != 1]
    late = [p for p in range(pairs) if p % 3 == 1]

    def grad_qkv(count, pair_at):
        @pl.loop(0, count)
        def _(n):
            cols = aligned(pair_at(n) * 6 * HEAD_DIM, 6 * HEAD_DIM, 128)
            wd[cols, :] = tn(proj[:, cols], normed_one[...]).astype(BF)

    if remote:
        reduce.feed(job_down + job_up)
    for n in range(3):
        attend_back(early, n * owned // 3, (n + 1) * owned // 3)
        if n < 2:
            tick()
    grad_qkv(len(early), lambda n: n + (n + 1) // 2)
    first_qkv = job_down + job_up + 1
    if remote:
        reduce.ready(first_qkv)
        reduce.ready(first_qkv + 1)
    tick()
    if remote:
        reduce.feed(first_qkv + 1)
    attend_back(late, 0, owned)
    grad_qkv(len(late), lambda n: 3 * n + 1)
    if remote:
        reduce.ready(first_qkv + 2)
    tick()
    if remote:
        reduce.feed(first_qkv + 2)
    if not remote:
        put_qkv = copy_in(wd, r["qkv_out_o"], sems.at[0])

    for n in range(3):
        blocks[1 + n].wait()
    token_copy(0, 0).start()

    def put_results(first, last):
        @pl.loop(first, last)
        def _(i):
            slot = lax.rem(i, 2)

            @pl.when(i + 1 < owned)
            def _():
                token_copy(i + 1, 1 - slot).start()

            rows = rows_of(i)
            rows_f = picked[rows, :].astype(F32)
            gate, valid = row_gate(rows_f, w_router, counts[i])
            branch = attn[rows, :]
            logit = valid * gate * (1.0 - gate) * jnp.sum(
                picked_grad[rows, :].astype(F32) * branch, axis=-1, keepdims=True
            )
            logits[rows, :] = jnp.broadcast_to(logit, (capacity, 128))
            vec[0, 4:5, :] += jnp.sum(logit * rows_f, axis=0, keepdims=True)
            table = slot_table(slot_row(i), length)
            upper, lower = split_low(gate * valid * branch)
            token_copy(i, slot).wait()

            @pl.when(i >= 2)
            def _():
                result_copy(i - 2, slot).wait()

            res[slot] = (tok[slot].astype(F32) + (nn(table, upper) + nn(table, lower))).astype(BF)
            result_copy(i, slot).start()

    put_results(0, owned // 2)
    tick()
    put_results(owned // 2, owned)

    @pl.loop(0, 3)
    def _(n):
        cols = aligned(n * width, width, 128)
        total = nn(proj[:, 0:features], rs[0:features, aligned(features + n * width, width, 128)])
        for k in range(1, 3):
            total += nn(
                proj[:, k * features : (k + 1) * features],
                rs[0:features, aligned((k + 1) * features + n * width, width, 128)],
            )
        attn[:, cols] = total

    cot_copy(0, 0).start()

    def put_gradients(first, last):
        @pl.loop(first, last)
        def _(i):
            slot = lax.rem(i, 2)

            @pl.when(i + 1 < owned)
            def _():
                cot_copy(i + 1, 1 - slot).start()

            rows = rows_of(i)
            rows_f = picked[rows, :].astype(F32)
            unit, scale = standardise(rows_f)
            grad = attn[rows, :]
            vec[0, 0:1, :] += jnp.sum(grad * unit, axis=0, keepdims=True)
            vec[0, 1:2, :] += jnp.sum(grad, axis=0, keepdims=True)
            back = norm_pull(grad, unit, scale, gain_one)
            total = back + wide[rows, :] + logits[rows, 0:1] * w_router
            table = slot_table(slot_row(i), length)
            upper, lower = split_low(total)
            cot_copy(i, slot).wait()

            @pl.when(i >= 2)
            def _():
                gtok_copy(i - 2, slot).wait()

            gtok[slot] = cot[slot].astype(F32) + (nn(table, upper) + nn(table, lower))
            gtok_copy(i, slot).start()

    put_gradients(0, owned // 2)
    tick()
    put_gradients(owned // 2, owned)

    if remote:
        stages = sum_vectors(place, vec, r["vec_in"], (r["vec_send"], r["vec_recv"]), reduce.sent)
        while ticks[0] < reduce.jobs + len(reduce.steps) - 1:
            if stages:
                stages.pop(0)()
            tick()
        while stages:
            stages.pop(0)()
        vec_o[...] = vec[vec.shape[0] - 1]
    else:
        vec_o[...] = vec[0]

    for i in range(max(owned - 2, 0), owned):
        result_copy(i, i % 2).wait()
        gtok_copy(i, i % 2).wait()
    if remote:
        reduce.close()
    else:
        put_down.wait()
        put_up.wait()
        put_qkv.wait()


def finish_kernel(sizes, *refs):
    grads, result, grad_tokens = refs[:3]
    outs, result_o, grad_tokens_o = refs[3:7], refs[7], refs[8]
    narrow, wide, kept_rows, kept_grads, in_sems, out_sems, row_sems = refs[9:]
    rows_in = [copy_in(result, kept_rows, row_sems.at[0]), copy_in(grad_tokens, kept_grads, row_sems.at[1])]
    chunk = 192
    places = [(out, r) for out, size in zip(outs, sizes) for r in range(0, size, chunk)]
    loads, copies = [], []
    for n in range(len(places)):
        rows = slice(n * chunk, (n + 1) * chunk)
        loads.append(copy_in(grads.at[rows], narrow.at[rows], in_sems.at[n]))
    for n, (out, r) in enumerate(places):
        rows = slice(n * chunk, (n + 1) * chunk)
        loads[n].wait()
        wide[rows, :] = narrow[rows, :].astype(F32)
        copies.append(copy_in(wide.at[rows], out.at[r : r + chunk], out_sems.at[n]))
        if n == 0:
            rows_in[0].wait()
            copies.append(copy_in(kept_rows, result_o, row_sems.at[2]))
            rows_in[1].wait()
            copies.append(copy_in(kept_grads, grad_tokens_o, row_sems.at[3]))
    for copy in copies:
        copy.wait()


def finish(grads, sizes, result, grad_tokens):
    total, features = grads.shape
    outside = pl.BlockSpec(memory_space=pltpu.HBM)
    S = jax.ShapeDtypeStruct
    D = pltpu.SemaphoreType.DMA
    shapes = [S((size, features), F32) for size in sizes]
    shapes += [S(result.shape, result.dtype), S(grad_tokens.shape, grad_tokens.dtype)]
    return pl.pallas_call(
        functools.partial(finish_kernel, sizes),
        out_shape=shapes,
        in_specs=[outside] * 3,
        out_specs=[outside] * len(shapes),
        scratch_shapes=[
            pltpu.VMEM((total, features), BF), pltpu.VMEM((total, features), F32),
            pltpu.VMEM(result.shape, BF), pltpu.VMEM(grad_tokens.shape, F32),
            D((total // 192,)), D((total // 192,)), D((4,)),
        ],
        compiler_params=pltpu.CompilerParams(vmem_limit_bytes=60 << 20),
    )(grads, result, grad_tokens)


def fused(
    parts, outer, tokens, slot_ids, counts, weights, w_up, w_down,
    gain_one, bias_one, gain_two, bias_two, w_router, cotangent,
):
    owned, length, features = tokens.shape
    capacity = slot_ids.shape[1]
    rows = owned * capacity
    hidden = w_up.shape[1]
    remote = outer > 0
    columns = weights[0].shape[0] * parts if remote else weights[0].shape[0] - features
    heads = columns // (3 * HEAD_DIM)
    S = jax.ShapeDtypeStruct
    inside = pl.BlockSpec(memory_space=pltpu.VMEM)
    outside = pl.BlockSpec(memory_space=pltpu.HBM)
    scalars = pl.BlockSpec(memory_space=pltpu.SMEM)
    V = pltpu.VMEM
    D = pltpu.SemaphoreType.DMA
    ins = {
        "slots": (slot_ids, inside), "counts": (counts, scalars),
        "gain_one": (gain_one, inside), "bias_one": (bias_one, inside), "gain_two": (gain_two, inside),
        "bias_two": (bias_two, inside), "w_router": (w_router, inside),
        "tokens": (tokens, outside), "cotangent": (cotangent, outside),
        "w_up": (w_up, outside), "w_down": (w_down, outside),
    }
    outs = {
        "result_o": (S((owned, length, features), BF), outside),
        "grad_tokens_o": (S((owned, length, features), F32), outside),
        "vec_o": (S((8, features), F32), inside),
        "saved_o": (S((rows, columns + features), BF), outside),
    }
    steps = 3
    if remote:
        steps = 5
    scratch = {
        "wu": V((features, hidden), BF), "wd": V((hidden, features), BF), "ra": V((rows, hidden), BF),
        "rs": V((rows, hidden), BF), "down": V((hidden, features), BF),
        "normed_two": V((rows, features), BF), "grad_mlp": V((rows, features), BF),
        "mixed": V((rows, features), BF), "attn": V((rows, features), F32), "wide": V((rows, features), F32),
        "picked": V((rows, features), BF), "picked_grad": V((rows, features), BF),
        "totals": V((owned, heads, capacity), F32), "logits": V((rows, 128), F32),
        "tok": V((2, length, features), BF), "cot": V((2, length, features), BF),
        "res": V((2, length, features), BF), "gtok": V((2, length, features), F32),
        "vec": V((steps + 1, 8, features), F32),
        "sems": D((10,)), "tok_sems": D((2,)), "cot_sems": D((2,)), "res_sems": D((2,)), "gtok_sems": D((2,)),
    }
    if remote:
        ins["w_qkv_t"] = (weights[0], outside)
        ins["w_out"] = (weights[1], outside)
        outs["w_saved_o"] = (S((columns + features, features), BF), outside)
        total = (columns + features + 2 * hidden) // parts
        jobs = 10
        outs["grads_o"] = (S((total, features), BF), outside)
        half = features // 2
        scratch.update({
            "from_core": V((2, total, features), BF), "from_x": V((total, features), BF),
            "from_y": V((total, half), BF), "from_low": V((total // 2, half), BF),
            "from_high": V((total // 4, half), BF),
            "vec_in": V((steps, 8, features), F32),
            "local_sems": D((2,)), "kept_sems": D((jobs,)),
        })
        for name, shape in (
            ("ag", (18,)), ("core", (jobs, 2)), ("x", (jobs,)), ("y", (jobs,)), ("z", (jobs, 2)),
            ("a", (jobs, 3)), ("vec", (steps,)),
        ):
            scratch[name + "_send"] = D(shape)
            scratch[name + "_recv"] = D(shape)
    else:
        ins["w_all"] = (weights[0], outside)
        outs["down_o"] = (S((hidden, features), BF), outside)
        outs["up_o"] = (S((features, hidden), BF), outside)
        outs["qkv_out_o"] = (S((columns + features, features), BF), outside)
    names = list(ins) + list(outs) + list(scratch)
    found = pl.pallas_call(
        functools.partial(fused_kernel, owned, length, capacity, parts, outer, names),
        out_shape=[v[0] for v in outs.values()],
        in_specs=[v[1] for v in ins.values()],
        out_specs=[v[1] for v in outs.values()],
        scratch_shapes=list(scratch.values()),
        compiler_params=pltpu.CompilerParams(
            vmem_limit_bytes=63 << 20,
            has_side_effects=remote,
            collective_id=0 if remote else None,
        ),
    )(*[v[0] for v in ins.values()])
    return dict(zip(outs, found))


def shards(
    images,
    tokens,
    slot_ids,
    counts,
    w_qkv,
    w_out,
    w_up,
    w_down,
    gain_one,
    bias_one,
    gain_two,
    bias_two,
    w_router,
    cotangent,
):
    features = tokens.shape[2]
    hidden = w_up.shape[1]
    parts = lax.axis_size("head")
    me = lax.axis_index("head")
    small = (gain_one, bias_one, gain_two, bias_two, w_router, cotangent)
    outer = images // 2 if images == 8 and parts == 4 else 0
    if outer:
        found = fused(
            parts, outer, tokens, slot_ids, counts, (w_qkv.T, w_out), w_up, w_down, *small
        )
        grads = found["grads_o"]
        part, rows = hidden // parts, w_out.shape[0]
        down, up, out, qkv, result, grad_tokens = finish(
            grads, (part, features, rows, grads.shape[0] - part - features - rows),
            found["result_o"], found["grad_tokens_o"],
        )
        qkv = qkv.T
        vectors = found["vec_o"]
    else:
        w_all = jnp.concatenate(
            [
                lax.all_gather(w_qkv.T, "head", axis=0, tiled=True),
                lax.all_gather(w_out, "head", axis=0, tiled=True),
            ]
        )
        found = fused(parts, outer, tokens, slot_ids, counts, (w_all,), w_up, w_down, *small)
        columns = w_all.shape[0] - features

        def reduced(matrix, axis=0):
            shard = lax.psum_scatter(matrix, "head", scatter_dimension=axis, tiled=True)
            piece = lax.psum_scatter(shard, "img", scatter_dimension=0, tiled=True)
            return lax.all_gather(piece, "img", axis=0, tiled=True).astype(F32)

        both = found["qkv_out_o"]
        down, up = reduced(found["down_o"]), reduced(found["up_o"], 1)
        out, qkv = reduced(both[columns:]), reduced(both[:columns]).T
        vectors = lax.psum(found["vec_o"], ("img", "head"))
        result, grad_tokens = found["result_o"], found["grad_tokens_o"]
    vectors = lax.dynamic_slice_in_dim(
        vectors, me * (features // parts), features // parts, axis=1
    )
    return (
        result,
        grad_tokens,
        qkv,
        out,
        up,
        down,
        vectors[0],
        vectors[1],
        vectors[2],
        vectors[3],
        vectors[4],
    )


def solution(mesh):
    return jax.shard_map(
        functools.partial(shards, mesh.shape["img"]),
        mesh=mesh,
        in_specs=(
            P(("img", "head"), None, None),
            P(("img", "head"), None),
            P(("img", "head")),
            P(None, "head"),
            P("head", None),
            P(),
            P(),
            P(),
            P(),
            P(),
            P(),
            P(),
            P(("img", "head"), None, None),
        ),
        out_specs=(
            P(("img", "head"), None, None),
            P(("img", "head"), None, None),
            P(None, "head"),
            P("head", None),
            P(None, "head"),
            P("head", None),
            P("head"),
            P("head"),
            P("head"),
            P("head"),
            P("head"),
        ),
        check_vma=False,
    )
```
